32 devices in a mesh: gx: 16 (over z, y, core), gy: 2 (over x).
Axes of the slice: x: 2, y: 2, z: 4, core: 2. Of those that a mesh axis runs over, the one named last changes fastest.
Arguments:
- adj_later: float32 [19, 128, 32, 256], P(None, 'gx', 'gy'), may hold values from -6 to 6
- saved_pops: bfloat16 [2, 19, 128, 32, 256], P(None, None, 'gx', 'gy'), may hold values from 0.015 to 0.49, as said below
- saved_scale: float32 [2, 19, 128, 32, 2], P(None, None, 'gx', 'gy'), may hold values from 0.7 to 1.4
- solid: int32 [128, 32, 256], P('gx', 'gy'), may hold values 0 or 1
- seed_values: float32 [4096, 19], P(('gx', 'gy')), may hold values from -12 to 12
- seed_contact: int32 [4096, 1], P(('gx', 'gy')), may hold values from 0 to 8; in each aligned block of 128 rows (0 to 127, 128 to 255, ...) at most 32 rows name the same one
- seed_cell: int32 [4096], P(('gx', 'gy')), may hold values from 0 to 32767
Outputs:
- adj_initial: float32 [19, 128, 32, 256], P(None, 'gx', 'gy')
- adj_middle: float32 [19, 128, 32, 256], P(None, 'gx', 'gy')
The draws below stay inside these ranges and needn't reach their ends.
Inputs may be any that keep to these rules, and one draw needn't show every extreme that they name: `saved_pops`: each saved population is its lattice weight w_i times a factor between 0.55 and 1.45. `seed_contact`: among the items held by one device no contact code appears more than 32 times; some code reaches 32 on some device.
All inputs are finite; a program needn't handle non-finite values. No bound on the sum of `solid` on one device may be relied on, other than what follows from the above.
Results may differ from the reference program's by a relative error of at most 0.0003.
Values sent between devices are 32-bit elements; how exact they have to be, the bound alone decides.
A program may use at most 128 MiB of HBM per device.

```python
import math
import jax
import jax.numpy as jnp
import numpy as np
from jax import lax

CX = 8
CY = 16
CZ = 256
ZB = 128
SURF_DEV = 128
CAP = 32
NX = 128
NY = 32
NZ = 256
NZB = 2
SURF_TOT = 4096
N_GX = 16
N_GY = 2


def draw_saved_pops(key, part):
    weights = jnp.array([1.0 / 3.0] + [1.0 / 18.0] * 6 + [1.0 / 36.0] * 12, jnp.float32).reshape(1, 19, 1, 1, 1)
    array_shape = (2, 19, NX, NY, NZ)
    jitter = jnp.clip(0.15 * jax.random.normal(key, array_shape, jnp.float32), -0.45, 0.45)
    return (weights * (1.0 + jitter)).astype(jnp.bfloat16)


def set_ends(entries, key, least, largest):
    extent = entries.shape
    index_at = [jax.random.randint(jax.random.fold_in(key, axis), (), 0, extent[axis]) for axis in range(len(extent))]
    entries = entries.at[tuple(index_at)].set(least)
    longest = extent.index(max(extent))
    index_at[longest] = (index_at[longest] + 1) % extent[longest]
    return entries.at[tuple(index_at)].set(largest)


def block_levels(stream_key, extent, pieces, smallest, top_value):
    def one(dim, parts):
        heights = jax.random.uniform(jax.random.fold_in(jax.random.fold_in(stream_key, 6), dim), (parts,), jnp.float32, smallest / len(pieces), top_value / len(pieces))
        return jnp.repeat(jnp.exp(heights), extent[dim] // parts).reshape((-1,) + (1,) * (len(extent) - dim - 1))

    loudness = one(*pieces[0])
    for cut in pieces[1:]:
        loudness = loudness * one(*cut)
    return loudness


def routed_block(rng, own, number, rows, count, top, limit, skew):
    sequence = jax.random.permutation(rng, count)
    packed, ordinary = portions_of(count, rows * top, limit, skew, True), portions_of(count, rows * top, limit, skew, False)
    places = jnp.arange(count)

    def named(tallies, turn):
        used = int((tallies > 0).sum())
        fixed = max(1, used // 4)
        moved = fixed + (places - fixed + turn * (used - fixed)) % max(1, count - fixed)
        return jnp.zeros((count,), jnp.int32).at[sequence[jnp.where(places < fixed, places, moved)]].set(jnp.asarray(tallies, jnp.int32))

    tallies = jnp.where(number % 4 == 0, named(packed, number // 4), named(ordinary, number - number // 4 - 1))
    mixed = jax.random.permutation(jax.random.fold_in(own, 3), count)
    source_of, sink = mixed[0:count // 2 * 2:2], mixed[1:count // 2 * 2:2]
    slack = jnp.minimum(tallies[source_of] - 1, limit - tallies[sink]) // 2
    slack = jnp.where((source_of == sequence[0]) | (sink == sequence[0]) | (tallies[sink] == 0), 0, jnp.maximum(slack, 0))
    moved = jax.random.randint(jax.random.fold_in(own, 4), (count // 2,), 0, 1 << 20) % (slack + 1)
    tallies = tallies.at[source_of].add(-moved).at[sink].add(moved)
    members = jnp.searchsorted(jnp.cumsum(tallies), jnp.arange(rows * top), side="right").astype(jnp.int32)
    grid = members.reshape(top, rows).T
    grid = grid[jax.random.permutation(jax.random.fold_in(own, 1), rows)]
    turn = jax.random.randint(jax.random.fold_in(own, 2), (rows, 1), 0, top)
    return jnp.take_along_axis(grid, (jnp.arange(top)[None, :] + turn) % top, axis=1)


def portions_of(count, total, most, lean, full):
    portions = [(1 << 20) // math.isqrt(grade ** lean) + 1 for grade in range(1, count + 1)]
    largest = most if full else min(most, max(-(-total // count), total * portions[0] // sum(portions)))
    least = 1 if total - largest >= count - 1 else 0
    given, surplus = [largest] + [least] * (count - 1), total - largest - least * (count - 1)
    while surplus > 0:
        movable = [i for i in range(1, count) if given[i] < largest] or [i for i in range(1, count) if given[i] < most]
        pool, budget = sum([portions[i] for i in movable]), surplus
        for i in movable:
            more = min(most - given[i], max(1, budget * portions[i] // pool), surplus)
            given[i] = given[i] + more
            surplus = surplus - more
    return np.array(given)


def gaussian(rng, shape, deviation, bound, pieces=(), kind=jnp.bfloat16):
    drawn = deviation * jax.random.normal(rng, shape, jnp.float32)
    if pieces:
        drawn = drawn * block_levels(rng, shape, pieces, -0.22, 0.18)
    return jnp.clip(drawn, -bound, bound).astype(kind)


def setup_inputs(seed: int = 0) -> dict:
    key_list = jax.random.split(jax.random.key(seed), 8)
    adj_later = gaussian(key_list[0], (19, NX, NY, NZ), 1.0, 6.0, ((1, 16), (2, 2)), jnp.float32)
    saved_pops = draw_saved_pops(jax.random.fold_in(key_list[7], 71), 0)
    saved_scale = jnp.clip(jnp.exp(math.log(1.4) - 0.6931472 * jax.random.uniform(key_list[2], (2, 19, NX, NY, NZB), jnp.float32) ** block_levels(key_list[2], (2, 19, NX, NY, NZB), ((2, 16), (3, 2)), -0.2, 0.2)), 0.7, 1.4)
    solid = set_ends((jax.random.randint(key_list[3], (NX, NY, NZ), 0, 5) < 1).astype(jnp.int32), jax.random.fold_in(key_list[3], 1), 0, 1)
    seed_values = gaussian(key_list[4], (SURF_TOT, 19), 3.0, 12.0, ((0, 32),), jnp.float32)
    seed_contact_keys = jax.random.split(jax.random.fold_in(key_list[5], 1), SURF_TOT // SURF_DEV)
    seed_contact_turns = jax.random.permutation(jax.random.fold_in(key_list[5], 3), SURF_TOT // SURF_DEV)
    seed_contact = jax.vmap(lambda own, number: routed_block(jax.random.fold_in(key_list[5], 2), own, number, SURF_DEV, 9, 1, CAP, 2))(seed_contact_keys, seed_contact_turns).reshape((SURF_TOT, 1))
    seed_cell = set_ends(jax.random.randint(key_list[6], (SURF_TOT,), 0, CX * CY * CZ), jax.random.fold_in(key_list[6], 1), 0, (CX * CY * CZ) - 1).astype(jnp.int32)
    return dict(adj_later=adj_later, saved_pops=saved_pops, saved_scale=saved_scale, solid=solid, seed_values=seed_values, seed_contact=seed_contact, seed_cell=seed_cell)


LATTICE = [(0, 0, 0), (1, 0, 0), (-1, 0, 0), (0, 1, 0), (0, -1, 0), (0, 0, 1), (0, 0, -1), (1, 1, 0), (-1, -1, 0), (1, -1, 0), (-1, 1, 0), (1, 0, 1), (-1, 0, -1), (1, 0, -1), (-1, 0, 1), (0, 1, 1), (0, -1, -1), (0, 1, -1), (0, -1, 1)]
OPPOSITE = [0, 2, 1, 4, 3, 6, 5, 8, 7, 10, 9, 12, 11, 14, 13, 16, 15, 18, 17]
LATTICE_WEIGHTS = [1.0 / 3.0] + [1.0 / 18.0] * 6 + [1.0 / 36.0] * 12
relaxation = 0.8

def collide(populations):
    lattice = jnp.array(LATTICE, jnp.float32).T
    weights = jnp.array(LATTICE_WEIGHTS, jnp.float32).reshape((19,) + (1,) * (populations.ndim - 1))
    density = lax.optimization_barrier(jnp.sum(populations, 0))
    momentum = jnp.einsum('ci,i...->c...', lattice, populations, precision=lax.Precision.HIGHEST)
    velocity = momentum / density
    projected = jnp.einsum('ci,c...->i...', lattice, velocity, precision=lax.Precision.HIGHEST)
    square = lax.optimization_barrier(jnp.sum(velocity * velocity, 0))
    equilibrium = weights * density * (1.0 + 3.0 * projected + 4.5 * projected * projected - 1.5 * square)
    return populations - (populations - equilibrium) / relaxation

def adjoint_collide(populations, adjoint, solid):
    unused, pull_back = jax.vjp(collide, populations)
    fluid_adjoint = pull_back(adjoint)[0]
    reversed_adjoint = jnp.stack([adjoint[other] for other in OPPOSITE])
    return jnp.where(solid[None] > 0, reversed_adjoint, fluid_adjoint)

def dequantize(quantized, scales):
    blocks = quantized.astype(jnp.float32).reshape(19, NX, NY, NZ // ZB, ZB)
    return (blocks * scales[..., None]).reshape(19, NX, NY, NZ)

def stream_back(adjoint):
    padded = jnp.pad(adjoint, ((0, 0), (1, 1), (1, 1), (1, 1)))
    slices = []
    for direction in range(19):
        step_x, step_y, step_z = LATTICE[direction]
        slices.append(padded[direction, 1 + step_x:1 + step_x + NX, 1 + step_y:1 + step_y + NY, 1 + step_z:1 + step_z + NZ])
    return jnp.stack(slices)

def adjoint_step(populations, adjoint, solid):
    read = jnp.moveaxis(stream_back(adjoint), 1, 0)
    pops_x = jnp.moveaxis(populations, 1, 0)
    result = lax.map(lambda group: adjoint_collide(group[0], group[1], group[2]), (pops_x, read, solid))
    return jnp.moveaxis(result, 0, 1)

def reference(adj_later, saved_pops, saved_scale, solid, seed_values, seed_contact, seed_cell):
    item_count = SURF_DEV * N_GX * N_GY
    source = jnp.arange(item_count, dtype=jnp.int32) // SURF_DEV
    contact = seed_contact[:, 0]
    target_x = source // N_GY + contact // 3 - 1
    target_y = source % N_GY + contact % 3 - 1
    valid = (target_x >= 0) & (target_x < N_GX) & (target_y >= 0) & (target_y < N_GY)
    global_x = jnp.clip(target_x, 0, N_GX - 1) * CX + seed_cell // (CY * CZ)
    global_y = jnp.clip(target_y, 0, N_GY - 1) * CY + seed_cell // CZ % CY
    global_z = seed_cell % CZ
    weighted = seed_values * valid[:, None].astype(jnp.float32)
    seed_field = jnp.zeros((19, NX, NY, NZ), jnp.float32).at[:, global_x, global_y, global_z].add(weighted.T)
    adjoint_end = adj_later + seed_field
    pops_late = dequantize(saved_pops[1], saved_scale[1])
    adj_middle = adjoint_step(pops_late, adjoint_end, solid)
    pops_early = dequantize(saved_pops[0], saved_scale[0])
    adj_initial = adjoint_step(pops_early, adj_middle, solid)
    return (adj_initial, adj_middle)
```

```python
import functools

import jax
import jax.numpy as jnp
from jax import lax
from jax.experimental import pallas as pl
from jax.experimental.pallas import tpu as pltpu
from jax.sharding import PartitionSpec as P

LATTICE = [
    (0, 0, 0),
    (1, 0, 0),
    (-1, 0, 0),
    (0, 1, 0),
    (0, -1, 0),
    (0, 0, 1),
    (0, 0, -1),
    (1, 1, 0),
    (-1, -1, 0),
    (1, -1, 0),
    (-1, 1, 0),
    (1, 0, 1),
    (-1, 0, -1),
    (1, 0, -1),
    (-1, 0, 1),
    (0, 1, 1),
    (0, -1, -1),
    (0, 1, -1),
    (0, -1, 1),
]
OPPOSITE = [0, 2, 1, 4, 3, 6, 5, 8, 7, 10, 9, 12, 11, 14, 13, 16, 15, 18, 17]
CAP = 32
MESH = pl.DeviceIdType.MESH
F32 = jnp.float32

ORDER = [1, 7, 9, 11, 13, 2, 8, 10, 12, 14, 0, 3, 4, 5, 6, 15, 16, 17, 18]
SLOT = [ORDER.index(pop) for pop in range(19)]
Y_SETS = [[3, 7, 10, 15, 17], [4, 8, 9, 16, 18]]


def velocities(pops, scale, step, x, out):
    rows, height = pops.shape[3], pops.shape[4]
    blocks = scale.shape[2] // rows
    factors = [scale[step, x, pl.ds(b, rows, stride=blocks), :] for b in range(blocks)]
    f = []
    for pop in range(19):
        wide = jnp.concatenate(
            [jnp.broadcast_to(c[:, pop : pop + 1], (rows, height // blocks)) for c in factors], 1
        )
        f.append(pops[step, pop, x].astype(F32) * wide)
    plus = {k: f[k] + f[k + 1] for k in range(1, 19, 2)}
    minus = {k: f[k] - f[k + 1] for k in range(1, 19, 2)}
    density = f[0]
    for k in range(1, 19, 2):
        density = density + plus[k]
    inverse = 1.0 / density
    out[step, 0, x] = (minus[1] + minus[7] + minus[9] + minus[11] + minus[13]) * inverse
    out[step, 1, x] = (minus[3] + minus[7] - minus[9] + minus[15] + minus[17]) * inverse
    out[step, 2, x] = (minus[5] + minus[11] - minus[13] + minus[15] - minus[17]) * inverse


def adjoint_plane(field, edge, velocity, solid, step, x, store):
    rows, height = field.shape[2], field.shape[3]
    row = lax.broadcasted_iota(jnp.int32, (rows, height), 0)
    col = lax.broadcasted_iota(jnp.int32, (rows, height), 1)
    h = []
    for pop in range(19):
        cx, cy, cz = LATTICE[pop]
        value = field[SLOT[pop], x + 1 + cx]
        if cy != 0:
            side = 0 if cy == 1 else 1
            place = Y_SETS[side].index(pop)
            line = edge[side, place, pl.ds(x + cx + 8, 1), :]
            turned = pltpu.roll(value, rows - 1 if cy == 1 else 1, 0)
            value = jnp.where(row == (rows - 1 if cy == 1 else 0), line, turned)
        if cz != 0:
            turned = pltpu.roll(value, height - 1 if cz == 1 else 1, 1)
            value = jnp.where(col == (height - 1 if cz == 1 else 0), 0.0, turned)
        h.append(value)
    s = {k: h[k] + h[k + 1] for k in range(1, 19, 2)}
    d = {k: h[k] - h[k + 1] for k in range(1, 19, 2)}
    diagonal = s[7] + s[9] + s[11] + s[13] + s[15] + s[17]
    total = 12.0 * h[0] + 2.0 * (s[1] + s[3] + s[5]) + diagonal
    ax = 2.0 * d[1] + d[7] + d[9] + d[11] + d[13]
    ay = 2.0 * d[3] + d[7] - d[9] + d[15] + d[17]
    az = 2.0 * d[5] + d[11] - d[13] + d[15] - d[17]
    bxx = 2.0 * s[1] + (s[7] + s[9]) + (s[11] + s[13])
    byy = 2.0 * s[3] + (s[7] + s[9]) + (s[15] + s[17])
    bzz = 2.0 * s[5] + (s[11] + s[13]) + (s[15] + s[17])
    bxy, bxz, byz = s[7] - s[9], s[11] - s[13], s[15] - s[17]
    ux, uy, uz = velocity[step, 0, x], velocity[step, 1, x], velocity[step, 2, x]
    qx = bxx * ux + bxy * uy + bxz * uz
    qy = bxy * ux + byy * uy + byz * uz
    qz = bxz * ux + byz * uy + bzz * uz
    square = ux * ux + uy * uy + uz * uz
    factor = 1.25 / 36.0
    base = (factor * total) * (1.0 + 1.5 * square) - (4.5 * factor) * (ux * qx + uy * qy + uz * qz)
    pull = (3.0 * factor) * total
    mx = (3.0 * factor) * ax + (9.0 * factor) * qx - pull * ux
    my = (3.0 * factor) * ay + (9.0 * factor) * qy - pull * uy
    mz = (3.0 * factor) * az + (9.0 * factor) * qz - pull * uz
    along = {
        1: mx, 3: my, 5: mz, 7: mx + my, 9: mx - my,
        11: mx + mz, 13: mx - mz, 15: my + mz, 17: my - mz,
    }
    is_solid = solid[x] > 0
    store(0, jnp.where(is_solid, h[0], base - 0.25 * h[0]))
    for k in range(1, 19, 2):
        store(k, jnp.where(is_solid, h[k + 1], (base + along[k]) - 0.25 * h[k]))
        store(k + 1, jnp.where(is_solid, h[k], (base - along[k]) - 0.25 * h[k + 1]))


def kernel(
    n_gx, n_gy, adj, pops_in, scale_in, solid_in, seed_values, contact, cell, out_init, out_mid,
    later, middle, initial, pops, scale, solid, velocity, item_out, item_in, item_all,
    z_hot, edge_out, edge, in_sem, out_sem, item_send, item_recv, face_send, face_recv,
):
    gx, gy = lax.axis_index("gx"), lax.axis_index("gy")
    wx, wy, height = adj.shape[1:]
    cells = wx * wy

    def here(ax, ay):
        px, py = gx + ax, gy + ay
        return (px >= 0) & (px < n_gx) & (py >= 0) & (py < n_gy)

    def at(ax, ay):
        return (gx + ax, gy + ay)

    around = [(ax, ay) for ax in (-1, 0, 1) for ay in (-1, 0, 1) if (ax, ay) != (0, 0)]

    copies = {}

    def fetch(name, index, source, target):
        copies[name] = pltpu.make_async_copy(source, target, in_sem.at[index])
        copies[name].start()

    fetch("pops1", 0, pops_in.at[1], pops.at[1])
    fetch("scale", 1, scale_in, scale)
    for slot in range(19):
        pltpu.make_async_copy(adj.at[ORDER[slot]], later.at[slot, pl.ds(1, wx)], in_sem.at[2]).start()
    fetch("solid", 3, solid_in, solid)
    fetch("pops0", 4, pops_in.at[0], pops.at[0])

    barrier = pltpu.get_barrier_semaphore()
    for ax, ay in around:
        @pl.when(here(ax, ay))
        def _(ax=ax, ay=ay):
            pl.semaphore_signal(barrier, inc=1, device_id=at(ax, ay), device_id_type=MESH)

    if n_gy == 2:
        other = 1 - 2 * gy
        routes = [(ax, rel) for ax in (-1, 0, 1) for rel in (0, 1)]
        shift_of = lambda rel: rel * other
    else:
        routes = [(ax, rel) for ax in (-1, 0, 1) for rel in (-1, 0, 1)]
        shift_of = lambda rel: rel
    back = {i: routes.index((-ax, rel if n_gy == 2 else -rel)) for i, (ax, rel) in enumerate(routes)}
    count = contact.shape[1]
    per_tile = 128 // CAP
    code = contact[...]
    code_across = jnp.broadcast_to(code, (count, count))
    first = lax.broadcasted_iota(jnp.int32, (count, count), 0)
    second = lax.broadcasted_iota(jnp.int32, (count, count), 1)
    same = (code_across == code_across.T) & (first < second)
    rank = jnp.sum(same.astype(jnp.int32), axis=0, keepdims=True)
    zeros = jnp.zeros((1, count), F32)
    values = [seed_values[pop : pop + 1, :] for pop in ORDER]
    top = jnp.concatenate(values + [zeros] * 5, 0)
    top_hi = top.astype(jnp.bfloat16)
    top_lo = (top - top_hi.astype(F32)).astype(jnp.bfloat16)
    place = cell[...]
    places = jnp.concatenate(
        [(place // height).astype(F32), (place % height).astype(F32)] + [zeros] * 14, 0
    ).astype(jnp.bfloat16)
    zero_rows = jnp.zeros((8, count), jnp.bfloat16)
    table = jnp.concatenate([top_hi, zero_rows, top_lo, zero_rows, places], 0)
    for i, (ax, rel) in enumerate(routes):
        lane = rank + CAP * (back[i] % per_tile)
        wanted = (ax + 1) * 3 + shift_of(rel) + 1
        lane = jnp.where(code == wanted, lane, -1)
        choose = (first == lane).astype(F32).astype(jnp.bfloat16)
        picked = lax.dot_general(
            table, choose, (((1,), (1,)), ((), ())), preferred_element_type=F32
        )
        tile = jnp.concatenate([picked[0:24] + picked[32:56], picked[64:72]], 0)
        if (ax, rel) == (0, 0):
            item_in[back[i]] = tile
        else:
            item_out[i] = tile

    def extent(position, size):
        return 1 + (position > 0).astype(jnp.int32) + (position < size - 1).astype(jnp.int32)

    pl.semaphore_wait(barrier, extent(gx, n_gx) * extent(gy, n_gy) - 1)

    def item_copy(i):
        ax, rel = routes[i]
        return pltpu.make_async_remote_copy(
            src_ref=item_out.at[i], dst_ref=item_in.at[back[i]],
            send_sem=item_send.at[i], recv_sem=item_recv.at[back[i]],
            device_id=at(ax, shift_of(rel)), device_id_type=MESH,
        )

    for i, (ax, rel) in enumerate(routes):
        if (ax, rel) != (0, 0):
            @pl.when(here(ax, shift_of(rel)))
            def _(i=i):
                item_copy(i).start()

            @pl.when(jnp.logical_not(here(ax, shift_of(rel))))
            def _(i=i):
                item_in[i] = jnp.zeros(item_in.shape[1:], F32)

    faces = ((later, 0), (middle, 1))
    for field, _ in faces:
        @pl.when(jnp.logical_not(here(1, 0)))
        def _(field=field):
            field[pl.ds(0, 5), wx + 1] = jnp.zeros((5, wy, height), F32)

        @pl.when(jnp.logical_not(here(-1, 0)))
        def _(field=field):
            field[pl.ds(5, 5), 0] = jnp.zeros((5, wy, height), F32)

    corners = []
    for side, ay in ((0, 1), (1, -1)):
        for pop in Y_SETS[side]:
            if LATTICE[pop][0] != 0:
                corners.append((side, Y_SETS[side].index(pop), LATTICE[pop][0], ay))
    for stage in range(2):
        for side, ay in ((0, 1), (1, -1)):
            @pl.when(jnp.logical_not(here(0, ay)))
            def _(stage=stage, side=side):
                edge[stage, side, :, pl.ds(8, wx), :] = jnp.zeros((5, wx, height), F32)
        for side, slot, cx, ay in corners:
            @pl.when(jnp.logical_not(here(cx, ay)))
            def _(stage=stage, side=side, slot=slot, cx=cx):
                edge[stage, side, slot, pl.ds(8 + 8 * cx, 8), :] = jnp.zeros((8, height), F32)

    def x_copy(stage, cx):
        field = faces[stage][0]
        pops_slot = pl.ds(0 if cx == 1 else 5, 5)
        near, far = (1, wx + 1) if cx == 1 else (wx, 0)
        index = 0 if cx == 1 else 1
        return pltpu.make_async_remote_copy(
            src_ref=field.at[pops_slot, near], dst_ref=field.at[pops_slot, far],
            send_sem=face_send.at[stage, index], recv_sem=face_recv.at[stage, index],
            device_id=at(-cx, 0), device_id_type=MESH,
        )

    def y_copy(stage, side):
        return pltpu.make_async_remote_copy(
            src_ref=edge_out.at[stage, side], dst_ref=edge.at[stage, side, :, pl.ds(8, wx), :],
            send_sem=face_send.at[stage, 2 + side], recv_sem=face_recv.at[stage, 2 + side],
            device_id=at(0, -1 if side == 0 else 1), device_id_type=MESH,
        )

    def corner_copy(stage, number):
        side, slot, cx, ay = corners[number]
        return pltpu.make_async_remote_copy(
            src_ref=edge_out.at[stage, side, slot],
            dst_ref=edge.at[stage, side, slot, pl.ds(8 + 8 * cx, 8), :],
            send_sem=face_send.at[stage, 4 + number], recv_sem=face_recv.at[stage, 4 + number],
            device_id=at(-cx, -ay), device_id_type=MESH,
        )

    x_links = [(lambda stage, cx=cx: x_copy(stage, cx), cx, 0) for cx in (1, -1)]
    y_links = [(lambda stage, side=side: y_copy(stage, side), 0, 1 if side == 0 else -1) for side in (0, 1)]
    y_links += [
        (lambda stage, number=number: corner_copy(stage, number), corners[number][2], corners[number][3])
        for number in range(4)
    ]

    def start(links, stage):
        for make, cx, cy in links:
            @pl.when(here(-cx, -cy))
            def _(make=make):
                make(stage).start()

    def arrive(links, stage):
        for make, cx, cy in links:
            @pl.when(here(cx, cy))
            def _(make=make):
                make(stage).wait_recv()

    def gather_edges(field, stage):
        for side in range(2):
            line = 0 if side == 0 else wy - 1
            for index, pop in enumerate(Y_SETS[side]):
                for x in range(wx):
                    edge_out[stage, side, index, x : x + 1, :] = field[SLOT[pop], 1 + x, line : line + 1, :]

    copies["pops1"].wait()
    copies["scale"].wait()

    def late(x, carry):
        velocities(pops, scale, 1, x, velocity)
        return carry

    lax.fori_loop(0, wx, late, 0)
    pltpu.make_async_copy(adj, later.at[:, pl.ds(1, wx)], in_sem.at[2]).wait()

    for i, (ax, rel) in enumerate(routes):
        if (ax, rel) != (0, 0):
            @pl.when(here(ax, shift_of(rel)))
            def _(i=i):
                pltpu.make_async_remote_copy(
                    src_ref=item_out.at[i], dst_ref=item_in.at[i],
                    send_sem=item_send.at[i], recv_sem=item_recv.at[i],
                    device_id=at(ax, shift_of(rel)), device_id_type=MESH,
                ).wait_recv()

    tiles = -(-len(routes) // per_tile)
    wide = tiles * 128
    gathered = []
    for t in range(tiles):
        part = item_in[t * per_tile]
        for i in range(t * per_tile + 1, min((t + 1) * per_tile, len(routes))):
            part = part + item_in[i]
        gathered.append(part)
    items = jnp.concatenate(gathered, 1)
    hi = items.astype(jnp.bfloat16).astype(F32)
    item_all[0] = hi
    item_all[1] = items - hi
    for t in range(tiles):
        z_row = jnp.broadcast_to(gathered[t][25:26, :], (128, 128))
        z_of = z_row.T.astype(jnp.int32)
        for b in range(height // 128):
            lanes = lax.broadcasted_iota(jnp.int32, (128, 128), 1) + 128 * b
            z_hot[pl.ds(128 * t, 128), pl.ds(128 * b, 128)] = (
                (z_of == lanes).astype(F32).astype(jnp.bfloat16)
            )
    xy_of = jnp.broadcast_to(items[24:25, :].astype(jnp.int32), (cells, wide))
    in_column = lax.broadcasted_iota(jnp.int32, (cells, wide), 0) == xy_of

    def add_seeds(slot, carry):
        spread = jnp.concatenate(
            [jnp.where(in_column, item_all[part, pl.ds(slot, 1), :], 0.0) for part in range(2)], 0
        ).astype(jnp.bfloat16)
        both = jnp.dot(spread, z_hot[...], preferred_element_type=F32)
        seeds = both[:cells] + both[cells:]
        later[slot, pl.ds(1, wx)] = later[slot, pl.ds(1, wx)] + seeds.reshape(wx, wy, height)
        return carry

    lax.fori_loop(0, 10, add_seeds, 0)
    start(x_links, 0)
    lax.fori_loop(10, 19, add_seeds, 0)
    gather_edges(later, 0)
    start(y_links, 0)

    copies["pops0"].wait()

    def early(x, carry):
        velocities(pops, scale, 0, x, velocity)
        return carry

    lax.fori_loop(0, wx, early, 0)
    copies["solid"].wait()

    def middle_plane(x):
        def store(pop, value):
            middle[SLOT[pop], x + 1] = value

        adjoint_plane(later, edge.at[0], velocity, solid, 1, x, store)

    def initial_plane(x):
        def store(pop, value):
            initial[pop, x] = value

        adjoint_plane(middle, edge.at[1], velocity, solid, 0, x, store)

    arrive(y_links, 0)
    arrive(x_links, 0)

    def ends(t, carry):
        middle_plane(t * (wx - 1))
        return carry

    lax.fori_loop(0, 2, ends, 0)
    start(x_links, 1)

    def inner(x, carry):
        middle_plane(x)
        return carry

    lax.fori_loop(1, wx - 1, inner, 0)
    gather_edges(middle, 1)
    start(y_links, 1)
    for slot in range(19):
        pltpu.make_async_copy(
            middle.at[slot, pl.ds(1, wx)], out_mid.at[ORDER[slot]], out_sem.at[0]
        ).start()

    def write(x):
        return pltpu.make_async_copy(initial.at[:, x], out_init.at[:, x], out_sem.at[1 + x])

    arrive(y_links, 1)

    def inner_last(x, carry):
        initial_plane(x)
        write(x).start()
        return carry

    lax.fori_loop(1, wx - 1, inner_last, 0)
    arrive(x_links, 1)

    def ends_last(t, carry):
        initial_plane(t * (wx - 1))
        write(t * (wx - 1)).start()
        return carry

    lax.fori_loop(0, 2, ends_last, 0)

    for i, (ax, rel) in enumerate(routes):
        if (ax, rel) != (0, 0):
            @pl.when(here(ax, shift_of(rel)))
            def _(i=i):
                item_copy(i).wait_send()
    for stage in range(2):
        for make, cx, cy in x_links + y_links:
            @pl.when(here(-cx, -cy))
            def _(make=make, stage=stage):
                make(stage).wait_send()
    pltpu.make_async_copy(middle.at[:, pl.ds(1, wx)], out_mid, out_sem.at[0]).wait()
    for x in range(wx):
        write(x).wait()


def body(n_gx, n_gy, adj_later, saved_pops, saved_scale, solid, seed_values, seed_contact, seed_cell):
    channels, wx, wy, height = adj_later.shape
    blocks = saved_scale.shape[-1]
    count = seed_cell.shape[0]
    scale = saved_scale.transpose(0, 2, 3, 4, 1).reshape(2, wx, wy * blocks, channels)
    routes = 6 if n_gy == 2 else 9
    wide = -(-routes * CAP // 128) * 128
    field = (channels, wx, wy, height)
    anywhere = pl.BlockSpec(memory_space=pl.ANY)
    in_vmem = pl.BlockSpec(memory_space=pltpu.VMEM)
    return pl.pallas_call(
        functools.partial(kernel, n_gx, n_gy),
        out_shape=[jax.ShapeDtypeStruct(field, F32)] * 2,
        in_specs=[anywhere] * 4 + [in_vmem] * 3,
        out_specs=[anywhere] * 2,
        scratch_shapes=[
            pltpu.VMEM((channels, wx + 2, wy, height), F32),
            pltpu.VMEM((channels, wx + 2, wy, height), F32),
            pltpu.VMEM(field, F32),
            pltpu.VMEM((2,) + field, jnp.bfloat16),
            pltpu.VMEM(scale.shape, F32),
            pltpu.VMEM((wx, wy, height), jnp.int32),
            pltpu.VMEM((2, 3, wx, wy, height), F32),
            pltpu.VMEM((routes, 32, 128), F32),
            pltpu.VMEM((routes, 32, 128), F32),
            pltpu.VMEM((2, 32, wide), F32),
            pltpu.VMEM((wide, height), jnp.bfloat16),
            pltpu.VMEM((2, 2, 5, wx, height), F32),
            pltpu.VMEM((2, 2, 5, wx + 16, height), F32),
            pltpu.SemaphoreType.DMA((5,)),
            pltpu.SemaphoreType.DMA((1 + wx,)),
            pltpu.SemaphoreType.DMA((routes,)),
            pltpu.SemaphoreType.DMA((routes,)),
            pltpu.SemaphoreType.DMA((2, 8)),
            pltpu.SemaphoreType.DMA((2, 8)),
        ],
        compiler_params=pltpu.CompilerParams(
            collective_id=0, has_side_effects=True, vmem_limit_bytes=40 * 1024 * 1024
        ),
    )(
        adj_later, saved_pops, scale, solid, seed_values.T,
        seed_contact.reshape(1, count), seed_cell.reshape(1, count),
    )


def solution(mesh):
    n_gx, n_gy = mesh.shape["gx"], mesh.shape["gy"]
    return jax.shard_map(
        functools.partial(body, n_gx, n_gy),
        mesh=mesh,
        in_specs=(
            P(None, "gx", "gy", None),
            P(None, None, "gx", "gy", None),
            P(None, None, "gx", "gy", None),
            P("gx", "gy", None),
            P(("gx", "gy"), None),
            P(("gx", "gy"), None),
            P(("gx", "gy")),
        ),
        out_specs=(P(None, "gx", "gy", None), P(None, "gx", "gy", None)),
        check_vma=False,
    )
```

```python
import functools

import jax
import jax.numpy as jnp
from jax import lax
from jax.experimental import pallas as pl
from jax.experimental.pallas import tpu as pltpu
from jax.sharding import PartitionSpec as P

LATTICE = [
    (0, 0, 0),
    (1, 0, 0),
    (-1, 0, 0),
    (0, 1, 0),
    (0, -1, 0),
    (0, 0, 1),
    (0, 0, -1),
    (1, 1, 0),
    (-1, -1, 0),
    (1, -1, 0),
    (-1, 1, 0),
    (1, 0, 1),
    (-1, 0, -1),
    (1, 0, -1),
    (-1, 0, 1),
    (0, 1, 1),
    (0, -1, -1),
    (0, 1, -1),
    (0, -1, 1),
]
OPPOSITE = [0, 2, 1, 4, 3, 6, 5, 8, 7, 10, 9, 12, 11, 14, 13, 16, 15, 18, 17]
CAP = 32
MESH = pl.DeviceIdType.MESH
F32 = jnp.float32

ORDER = [1, 7, 9, 11, 13, 2, 8, 10, 12, 14, 0, 3, 4, 5, 6, 15, 16, 17, 18]
SLOT = [ORDER.index(pop) for pop in range(19)]
Y_SETS = [[3, 7, 10, 15, 17], [4, 8, 9, 16, 18]]


def velocities(pops, scale, step, x, out):
    rows, height = pops.shape[3], pops.shape[4]
    blocks = scale.shape[2] // rows
    factors = [scale[step, x, pl.ds(b, rows, stride=blocks), :] for b in range(blocks)]
    f = []
    for pop in range(19):
        wide = jnp.concatenate(
            [jnp.broadcast_to(c[:, pop : pop + 1], (rows, height // blocks)) for c in factors], 1
        )
        f.append(pops[step, pop, x].astype(F32) * wide)
    plus = {k: f[k] + f[k + 1] for k in range(1, 19, 2)}
    minus = {k: f[k] - f[k + 1] for k in range(1, 19, 2)}
    density = f[0]
    for k in range(1, 19, 2):
        density = density + plus[k]
    inverse = 1.0 / density
    out[step, 0, x] = (minus[1] + minus[7] + minus[9] + minus[11] + minus[13]) * inverse
    out[step, 1, x] = (minus[3] + minus[7] - minus[9] + minus[15] + minus[17]) * inverse
    out[step, 2, x] = (minus[5] + minus[11] - minus[13] + minus[15] - minus[17]) * inverse


def adjoint_plane(field, edge, velocity, solid, step, x, store):
    rows, height = field.shape[2], field.shape[3]
    row = lax.broadcasted_iota(jnp.int32, (rows, height), 0)
    col = lax.broadcasted_iota(jnp.int32, (rows, height), 1)
    h = []
    for pop in range(19):
        cx, cy, cz = LATTICE[pop]
        value = field[SLOT[pop], x + 1 + cx]
        if cy != 0:
            side = 0 if cy == 1 else 1
            place = Y_SETS[side].index(pop)
            line = edge[side, place, pl.ds(x + cx + 8, 1), :]
            turned = pltpu.roll(value, rows - 1 if cy == 1 else 1, 0)
            value = jnp.where(row == (rows - 1 if cy == 1 else 0), line, turned)
        if cz != 0:
            turned = pltpu.roll(value, height - 1 if cz == 1 else 1, 1)
            value = jnp.where(col == (height - 1 if cz == 1 else 0), 0.0, turned)
        h.append(value)
    s = {k: h[k] + h[k + 1] for k in range(1, 19, 2)}
    d = {k: h[k] - h[k + 1] for k in range(1, 19, 2)}
    diagonal = s[7] + s[9] + s[11] + s[13] + s[15] + s[17]
    total = 12.0 * h[0] + 2.0 * (s[1] + s[3] + s[5]) + diagonal
    ax = 2.0 * d[1] + d[7] + d[9] + d[11] + d[13]
    ay = 2.0 * d[3] + d[7] - d[9] + d[15] + d[17]
    az = 2.0 * d[5] + d[11] - d[13] + d[15] - d[17]
    bxx = 2.0 * s[1] + (s[7] + s[9]) + (s[11] + s[13])
    byy = 2.0 * s[3] + (s[7] + s[9]) + (s[15] + s[17])
    bzz = 2.0 * s[5] + (s[11] + s[13]) + (s[15] + s[17])
    bxy, bxz, byz = s[7] - s[9], s[11] - s[13], s[15] - s[17]
    ux, uy, uz = velocity[step, 0, x], velocity[step, 1, x], velocity[step, 2, x]
    qx = bxx * ux + bxy * uy + bxz * uz
    qy = bxy * ux + byy * uy + byz * uz
    qz = bxz * ux + byz * uy + bzz * uz
    square = ux * ux + uy * uy + uz * uz
    factor = 1.25 / 36.0
    base = (factor * total) * (1.0 + 1.5 * square) - (4.5 * factor) * (ux * qx + uy * qy + uz * qz)
    pull = (3.0 * factor) * total
    mx = (3.0 * factor) * ax + (9.0 * factor) * qx - pull * ux
    my = (3.0 * factor) * ay + (9.0 * factor) * qy - pull * uy
    mz = (3.0 * factor) * az + (9.0 * factor) * qz - pull * uz
    along = {
        1: mx, 3: my, 5: mz, 7: mx + my, 9: mx - my,
        11: mx + mz, 13: mx - mz, 15: my + mz, 17: my - mz,
    }
    is_solid = solid[x] > 0
    store(0, jnp.where(is_solid, h[0], base - 0.25 * h[0]))
    for k in range(1, 19, 2):
        store(k, jnp.where(is_solid, h[k + 1], (base + along[k]) - 0.25 * h[k]))
        store(k + 1, jnp.where(is_solid, h[k], (base - along[k]) - 0.25 * h[k + 1]))


def kernel(
    n_gx, n_gy, adj, pops_in, scale_in, solid_in, values_in, contact_in, cell_in, out_init, out_mid,
    later, middle, initial, pops, scale, solid, velocity, seed_values, contact, cell,
    item_out, item_in, item_all, z_hot, face_out, edge_out, edge, in_sem, out_sem, item_send, item_recv, face_send, face_recv,
):
    gx, gy = lax.axis_index("gx"), lax.axis_index("gy")
    wx, wy, height = adj.shape[1:]
    cells = wx * wy

    def here(ax, ay):
        px, py = gx + ax, gy + ay
        return (px >= 0) & (px < n_gx) & (py >= 0) & (py < n_gy)

    def at(ax, ay):
        return (gx + ax, gy + ay)

    around = [(ax, ay) for ax in (-1, 0, 1) for ay in (-1, 0, 1) if (ax, ay) != (0, 0)]

    copies = {}

    def fetch(name, index, source, target):
        copies[name] = pltpu.make_async_copy(source, target, in_sem.at[index])
        copies[name].start()

    fetch("contact", 5, contact_in, contact)
    fetch("cell", 6, cell_in, cell)
    fetch("values", 7, values_in, seed_values)
    fetch("pops1", 0, pops_in.at[1], pops.at[1])
    fetch("scale", 1, scale_in, scale)
    for slot in range(19):
        pltpu.make_async_copy(adj.at[ORDER[slot]], later.at[slot, pl.ds(1, wx)], in_sem.at[2]).start()
    fetch("solid", 3, solid_in, solid)
    fetch("pops0", 4, pops_in.at[0], pops.at[0])

    barrier = pltpu.get_barrier_semaphore()
    for ax, ay in around:
        @pl.when(here(ax, ay))
        def _(ax=ax, ay=ay):
            pl.semaphore_signal(barrier, inc=1, device_id=at(ax, ay), device_id_type=MESH)

    if n_gy == 2:
        other = 1 - 2 * gy
        routes = [(ax, rel) for ax in (-1, 0, 1) for rel in (0, 1)]
        shift_of = lambda rel: rel * other
    else:
        routes = [(ax, rel) for ax in (-1, 0, 1) for rel in (-1, 0, 1)]
        shift_of = lambda rel: rel
    back = {i: routes.index((-ax, rel if n_gy == 2 else -rel)) for i, (ax, rel) in enumerate(routes)}
    for name in ("contact", "cell", "values"):
        copies[name].wait()
    count = contact.shape[1]
    per_tile = 128 // CAP
    code = contact[...]
    code_across = jnp.broadcast_to(code, (count, count))
    first = lax.broadcasted_iota(jnp.int32, (count, count), 0)
    second = lax.broadcasted_iota(jnp.int32, (count, count), 1)
    same = (code_across == code_across.T) & (first < second)
    rank = jnp.sum(same.astype(jnp.int32), axis=0, keepdims=True)
    zeros = jnp.zeros((1, count), F32)
    values = [seed_values[pop : pop + 1, :] for pop in ORDER]
    top = jnp.concatenate(values + [zeros] * 5, 0)
    top_hi = top.astype(jnp.bfloat16)
    top_lo = (top - top_hi.astype(F32)).astype(jnp.bfloat16)
    place = cell[...]
    places = jnp.concatenate(
        [(place // height).astype(F32), (place % height).astype(F32)] + [zeros] * 14, 0
    ).astype(jnp.bfloat16)
    zero_rows = jnp.zeros((8, count), jnp.bfloat16)
    table = jnp.concatenate([top_hi, zero_rows, top_lo, zero_rows, places], 0)
    for i, (ax, rel) in enumerate(routes):
        lane = rank + CAP * (back[i] % per_tile)
        wanted = (ax + 1) * 3 + shift_of(rel) + 1
        lane = jnp.where(code == wanted, lane, -1)
        choose = (first == lane).astype(F32).astype(jnp.bfloat16)
        picked = lax.dot_general(
            table, choose, (((1,), (1,)), ((), ())), preferred_element_type=F32
        )
        tile = jnp.concatenate([picked[0:24] + picked[32:56], picked[64:72]], 0)
        if (ax, rel) == (0, 0):
            item_in[back[i]] = tile
        else:
            item_out[i] = tile

    def extent(position, size):
        return 1 + (position > 0).astype(jnp.int32) + (position < size - 1).astype(jnp.int32)

    pl.semaphore_wait(barrier, extent(gx, n_gx) * extent(gy, n_gy) - 1)

    def item_copy(i):
        ax, rel = routes[i]
        return pltpu.make_async_remote_copy(
            src_ref=item_out.at[i], dst_ref=item_in.at[back[i]],
            send_sem=item_send.at[i], recv_sem=item_recv.at[back[i]],
            device_id=at(ax, shift_of(rel)), device_id_type=MESH,
        )

    for i, (ax, rel) in enumerate(routes):
        if (ax, rel) != (0, 0):
            @pl.when(here(ax, shift_of(rel)))
            def _(i=i):
                item_copy(i).start()

            @pl.when(jnp.logical_not(here(ax, shift_of(rel))))
            def _(i=i):
                item_in[i] = jnp.zeros(item_in.shape[1:], F32)

    faces = ((later, 0), (middle, 1))
    for field, _ in faces:
        @pl.when(jnp.logical_not(here(1, 0)))
        def _(field=field):
            field[pl.ds(0, 5), wx + 1] = jnp.zeros((5, wy, height), F32)

        @pl.when(jnp.logical_not(here(-1, 0)))
        def _(field=field):
            field[pl.ds(5, 5), 0] = jnp.zeros((5, wy, height), F32)

    corners = []
    for side, ay in ((0, 1), (1, -1)):
        for pop in Y_SETS[side]:
            if LATTICE[pop][0] != 0:
                corners.append((side, Y_SETS[side].index(pop), LATTICE[pop][0], ay))
    for stage in range(2):
        for side, ay in ((0, 1), (1, -1)):
            @pl.when(jnp.logical_not(here(0, ay)))
            def _(stage=stage, side=side):
                edge[stage, side, :, pl.ds(8, wx), :] = jnp.zeros((5, wx, height), F32)
        for side, slot, cx, ay in corners:
            @pl.when(jnp.logical_not(here(cx, ay)))
            def _(stage=stage, side=side, slot=slot, cx=cx):
                edge[stage, side, slot, pl.ds(8 + 8 * cx, 8), :] = jnp.zeros((8, height), F32)

    def x_copy(stage, cx):
        field = faces[stage][0]
        pops_slot = pl.ds(0 if cx == 1 else 5, 5)
        near, far = (1, wx + 1) if cx == 1 else (wx, 0)
        index = 0 if cx == 1 else 1
        return pltpu.make_async_remote_copy(
            src_ref=face_out.at[index] if stage == 0 else field.at[pops_slot, near],
            dst_ref=field.at[pops_slot, far],
            send_sem=face_send.at[stage, index], recv_sem=face_recv.at[stage, index],
            device_id=at(-cx, 0), device_id_type=MESH,
        )

    def y_copy(stage, side):
        return pltpu.make_async_remote_copy(
            src_ref=edge_out.at[stage, side], dst_ref=edge.at[stage, side, :, pl.ds(8, wx), :],
            send_sem=face_send.at[stage, 2 + side], recv_sem=face_recv.at[stage, 2 + side],
            device_id=at(0, -1 if side == 0 else 1), device_id_type=MESH,
        )

    def corner_copy(stage, number):
        side, slot, cx, ay = corners[number]
        return pltpu.make_async_remote_copy(
            src_ref=edge_out.at[stage, side, slot],
            dst_ref=edge.at[stage, side, slot, pl.ds(8 + 8 * cx, 8), :],
            send_sem=face_send.at[stage, 4 + number], recv_sem=face_recv.at[stage, 4 + number],
            device_id=at(-cx, -ay), device_id_type=MESH,
        )

    x_links = [(lambda stage, cx=cx: x_copy(stage, cx), cx, 0) for cx in (1, -1)]
    y_links = [(lambda stage, side=side: y_copy(stage, side), 0, 1 if side == 0 else -1) for side in (0, 1)]
    y_links += [
        (lambda stage, number=number: corner_copy(stage, number), corners[number][2], corners[number][3])
        for number in range(4)
    ]

    def start(links, stage):
        for make, cx, cy in links:
            @pl.when(here(-cx, -cy))
            def _(make=make):
                make(stage).start()

    def arrive(links, stage):
        for make, cx, cy in links:
            @pl.when(here(cx, cy))
            def _(make=make):
                make(stage).wait_recv()

    copies["pops1"].wait()
    copies["scale"].wait()

    def late(x, carry):
        velocities(pops, scale, 1, x, velocity)
        return carry

    lax.fori_loop(0, wx, late, 0)
    pltpu.make_async_copy(adj, later.at[:, pl.ds(1, wx)], in_sem.at[2]).wait()
    for side in range(2):
        line = 0 if side == 0 else wy - 1
        for index, pop in enumerate(Y_SETS[side]):
            for x in range(wx):
                edge_out[0, side, index, x : x + 1, :] = later[SLOT[pop], 1 + x, line : line + 1, :]

    for i, (ax, rel) in enumerate(routes):
        if (ax, rel) != (0, 0):
            @pl.when(here(ax, shift_of(rel)))
            def _(i=i):
                pltpu.make_async_remote_copy(
                    src_ref=item_out.at[i], dst_ref=item_in.at[i],
                    send_sem=item_send.at[i], recv_sem=item_recv.at[i],
                    device_id=at(ax, shift_of(rel)), device_id_type=MESH,
                ).wait_recv()

    tiles = -(-len(routes) // per_tile)
    wide = tiles * 128
    gathered = []
    for t in range(tiles):
        part = item_in[t * per_tile]
        for i in range(t * per_tile + 1, min((t + 1) * per_tile, len(routes))):
            part = part + item_in[i]
        gathered.append(part)
    items = jnp.concatenate(gathered, 1)
    hi = items.astype(jnp.bfloat16).astype(F32)
    item_all[0] = hi
    item_all[1] = items - hi
    for t in range(tiles):
        z_row = jnp.broadcast_to(gathered[t][25:26, :], (128, 128))
        z_of = z_row.T.astype(jnp.int32)
        for b in range(height // 128):
            lanes = lax.broadcasted_iota(jnp.int32, (128, 128), 1) + 128 * b
            z_hot[pl.ds(128 * t, 128), pl.ds(128 * b, 128)] = (
                (z_of == lanes).astype(F32).astype(jnp.bfloat16)
            )
    xy_of = items[24:25, :].astype(jnp.int32)

    def at_cells(length, first, stride):
        number = lax.broadcasted_iota(jnp.int32, (length, wide), 0)
        return number * stride + first == jnp.broadcast_to(xy_of, (length, wide))

    def field_of(rows):
        spread = jnp.concatenate(
            [
                jnp.where(match, item_all[part, slot : slot + 1, :], 0.0)
                for part in range(2)
                for slot, match in rows
            ],
            0,
        ).astype(jnp.bfloat16)
        both = jnp.dot(spread, z_hot[...], preferred_element_type=F32)
        half = both.shape[0] // 2
        return both[:half] + both[half:]

    near = [at_cells(wy, 0, 1), at_cells(wy, (wx - 1) * wy, 1)]
    line_of = [at_cells(wx, 0, wy), at_cells(wx, wy - 1, wy)]
    rows = [(5 * i + j, near[i]) for i in range(2) for j in range(5)]
    rows += [(SLOT[pop], line_of[side]) for side in range(2) for pop in Y_SETS[side]]
    outer = field_of(rows)
    for i in range(2):
        plane = later[pl.ds(5 * i, 5), 1 if i == 0 else wx]
        face_out[i] = plane + outer[5 * wy * i : 5 * wy * (i + 1)].reshape(5, wy, height)
    start(x_links, 0)
    begin = 10 * wy
    for side in range(2):
        part = outer[begin + 5 * wx * side : begin + 5 * wx * (side + 1)]
        edge_out[0, side] = edge_out[0, side] + part.reshape(5, wx, height)
    start(y_links, 0)

    def add_seeds(x, carry):
        match = at_cells(wy, x * wy, 1)
        seeds = field_of([(slot, match) for slot in range(19)])
        later[:, x + 1] = later[:, x + 1] + seeds.reshape(19, wy, height)
        return carry

    lax.fori_loop(0, wx, add_seeds, 0)
    copies["solid"].wait()

    def middle_plane(x):
        def store(pop, value):
            middle[SLOT[pop], x + 1] = value
            cy = LATTICE[pop][1]
            if cy != 0:
                side, line = (0, 0) if cy == 1 else (1, wy - 1)
                edge_out[1, side, Y_SETS[side].index(pop), pl.ds(x, 1), :] = value[line : line + 1, :]

        adjoint_plane(later, edge.at[0], velocity, solid, 1, x, store)

    def initial_plane(x):
        def store(pop, value):
            initial[pop, x] = value

        adjoint_plane(middle, edge.at[1], velocity, solid, 0, x, store)

    arrive(y_links, 0)
    arrive(x_links, 0)

    def ends(t, carry):
        middle_plane(t * (wx - 1))
        return carry

    lax.fori_loop(0, 2, ends, 0)
    start(x_links, 1)

    def inner(x, carry):
        middle_plane(x)
        return carry

    lax.fori_loop(1, wx - 1, inner, 0)
    start(y_links, 1)
    for slot in range(19):
        pltpu.make_async_copy(
            middle.at[slot, pl.ds(1, wx)], out_mid.at[ORDER[slot]], out_sem.at[0]
        ).start()

    def write(x):
        return pltpu.make_async_copy(initial.at[:, x], out_init.at[:, x], out_sem.at[1 + x])

    copies["pops0"].wait()

    def early(x, carry):
        velocities(pops, scale, 0, x, velocity)
        return carry

    lax.fori_loop(0, wx, early, 0)
    arrive(y_links, 1)

    def inner_last(x, carry):
        initial_plane(x)
        write(x).start()
        return carry

    lax.fori_loop(1, wx - 1, inner_last, 0)
    arrive(x_links, 1)

    def ends_last(t, carry):
        initial_plane(t * (wx - 1))
        write(t * (wx - 1)).start()
        return carry

    lax.fori_loop(0, 2, ends_last, 0)

    for i, (ax, rel) in enumerate(routes):
        if (ax, rel) != (0, 0):
            @pl.when(here(ax, shift_of(rel)))
            def _(i=i):
                item_copy(i).wait_send()
    for stage in range(2):
        for make, cx, cy in x_links + y_links:
            @pl.when(here(-cx, -cy))
            def _(make=make, stage=stage):
                make(stage).wait_send()
    pltpu.make_async_copy(middle.at[:, pl.ds(1, wx)], out_mid, out_sem.at[0]).wait()
    for x in range(wx):
        write(x).wait()


def body(n_gx, n_gy, adj_later, saved_pops, saved_scale, solid, seed_values, seed_contact, seed_cell):
    channels, wx, wy, height = adj_later.shape
    blocks = saved_scale.shape[-1]
    count = seed_cell.shape[0]
    scale = saved_scale.transpose(0, 2, 3, 4, 1).reshape(2, wx, wy * blocks, channels)
    routes = 6 if n_gy == 2 else 9
    wide = -(-routes * CAP // 128) * 128
    field = (channels, wx, wy, height)
    in_hbm = pl.BlockSpec(memory_space=pltpu.HBM)
    return pl.pallas_call(
        functools.partial(kernel, n_gx, n_gy),
        out_shape=[jax.ShapeDtypeStruct(field, F32)] * 2,
        in_specs=[in_hbm] * 7,
        out_specs=[in_hbm] * 2,
        scratch_shapes=[
            pltpu.VMEM((channels, wx + 2, wy, height), F32),
            pltpu.VMEM((channels, wx + 2, wy, height), F32),
            pltpu.VMEM(field, F32),
            pltpu.VMEM((2,) + field, jnp.bfloat16),
            pltpu.VMEM(scale.shape, F32),
            pltpu.VMEM((wx, wy, height), jnp.int32),
            pltpu.VMEM((2, 3, wx, wy, height), F32),
            pltpu.VMEM((channels, count), F32),
            pltpu.VMEM((1, count), jnp.int32),
            pltpu.VMEM((1, count), jnp.int32),
            pltpu.VMEM((routes, 32, 128), F32),
            pltpu.VMEM((routes, 32, 128), F32),
            pltpu.VMEM((2, 32, wide), F32),
            pltpu.VMEM((wide, height), jnp.bfloat16),
            pltpu.VMEM((2, 5, wy, height), F32),
            pltpu.VMEM((2, 2, 5, wx, height), F32),
            pltpu.VMEM((2, 2, 5, wx + 16, height), F32),
            pltpu.SemaphoreType.DMA((8,)),
            pltpu.SemaphoreType.DMA((1 + wx,)),
            pltpu.SemaphoreType.DMA((routes,)),
            pltpu.SemaphoreType.DMA((routes,)),
            pltpu.SemaphoreType.DMA((2, 8)),
            pltpu.SemaphoreType.DMA((2, 8)),
        ],
        compiler_params=pltpu.CompilerParams(
            collective_id=0, has_side_effects=True, vmem_limit_bytes=60 * 1024 * 1024
        ),
    )(
        adj_later, saved_pops, scale, solid, seed_values.T,
        seed_contact.reshape(1, count), seed_cell.reshape(1, count),
    )


def solution(mesh):
    n_gx, n_gy = mesh.shape["gx"], mesh.shape["gy"]
    return jax.shard_map(
        functools.partial(body, n_gx, n_gy),
        mesh=mesh,
        in_specs=(
            P(None, "gx", "gy", None),
            P(None, None, "gx", "gy", None),
            P(None, None, "gx", "gy", None),
            P("gx", "gy", None),
            P(("gx", "gy"), None),
            P(("gx", "gy"), None),
            P(("gx", "gy")),
        ),
        out_specs=(P(None, "gx", "gy", None), P(None, "gx", "gy", None)),
        check_vma=False,
    )
```

```python
import functools

import jax
import jax.numpy as jnp
from jax import lax
from jax.experimental import pallas as pl
from jax.experimental.pallas import tpu as pltpu
from jax.sharding import PartitionSpec as P

LATTICE = [
    (0, 0, 0),
    (1, 0, 0),
    (-1, 0, 0),
    (0, 1, 0),
    (0, -1, 0),
    (0, 0, 1),
    (0, 0, -1),
    (1, 1, 0),
    (-1, -1, 0),
    (1, -1, 0),
    (-1, 1, 0),
    (1, 0, 1),
    (-1, 0, -1),
    (1, 0, -1),
    (-1, 0, 1),
    (0, 1, 1),
    (0, -1, -1),
    (0, 1, -1),
    (0, -1, 1),
]
OPPOSITE = [0, 2, 1, 4, 3, 6, 5, 8, 7, 10, 9, 12, 11, 14, 13, 16, 15, 18, 17]
CAP = 32
MESH = pl.DeviceIdType.MESH
F32 = jnp.float32

ORDER = [1, 7, 9, 11, 13, 2, 8, 10, 12, 14, 0, 3, 4, 5, 6, 15, 16, 17, 18]
SLOT = [ORDER.index(pop) for pop in range(19)]
Y_SETS = [[3, 7, 10, 15, 17], [4, 8, 9, 16, 18]]


def velocities(pops, scale, step, x, out):
    rows, height = pops.shape[3], pops.shape[4]
    blocks = scale.shape[2] // rows
    factors = [scale[step, x, pl.ds(b, rows, stride=blocks), :] for b in range(blocks)]
    f = []
    for pop in range(19):
        wide = jnp.concatenate(
            [jnp.broadcast_to(c[:, pop : pop + 1], (rows, height // blocks)) for c in factors], 1
        )
        f.append(pops[step, pop, x].astype(F32) * wide)
    plus = {k: f[k] + f[k + 1] for k in range(1, 19, 2)}
    minus = {k: f[k] - f[k + 1] for k in range(1, 19, 2)}
    density = f[0]
    for k in range(1, 19, 2):
        density = density + plus[k]
    inverse = 1.0 / density
    out[step, 0, x] = (minus[1] + minus[7] + minus[9] + minus[11] + minus[13]) * inverse
    out[step, 1, x] = (minus[3] + minus[7] - minus[9] + minus[15] + minus[17]) * inverse
    out[step, 2, x] = (minus[5] + minus[11] - minus[13] + minus[15] - minus[17]) * inverse


def adjoint_plane(field, slots, edge, velocity, solid, x, store):
    rows, height = field.shape[2], field.shape[3]
    row = lax.broadcasted_iota(jnp.int32, (rows, height), 0)
    col = lax.broadcasted_iota(jnp.int32, (rows, height), 1)
    h = []
    for pop in range(19):
        cx, cy, cz = LATTICE[pop]
        value = field[slots[pop], x + 1 + cx]
        if cy != 0:
            side = 0 if cy == 1 else 1
            place = Y_SETS[side].index(pop)
            line = edge[side, place, pl.ds(x + cx + 8, 1), :]
            turned = pltpu.roll(value, rows - 1 if cy == 1 else 1, 0)
            value = jnp.where(row == (rows - 1 if cy == 1 else 0), line, turned)
        if cz != 0:
            turned = pltpu.roll(value, height - 1 if cz == 1 else 1, 1)
            value = jnp.where(col == (height - 1 if cz == 1 else 0), 0.0, turned)
        h.append(value)
    s = {k: h[k] + h[k + 1] for k in range(1, 19, 2)}
    d = {k: h[k] - h[k + 1] for k in range(1, 19, 2)}
    diagonal = s[7] + s[9] + s[11] + s[13] + s[15] + s[17]
    total = 12.0 * h[0] + 2.0 * (s[1] + s[3] + s[5]) + diagonal
    ax = 2.0 * d[1] + d[7] + d[9] + d[11] + d[13]
    ay = 2.0 * d[3] + d[7] - d[9] + d[15] + d[17]
    az = 2.0 * d[5] + d[11] - d[13] + d[15] - d[17]
    bxx = 2.0 * s[1] + (s[7] + s[9]) + (s[11] + s[13])
    byy = 2.0 * s[3] + (s[7] + s[9]) + (s[15] + s[17])
    bzz = 2.0 * s[5] + (s[11] + s[13]) + (s[15] + s[17])
    bxy, bxz, byz = s[7] - s[9], s[11] - s[13], s[15] - s[17]
    ux, uy, uz = velocity[0, x], velocity[1, x], velocity[2, x]
    qx = bxx * ux + bxy * uy + bxz * uz
    qy = bxy * ux + byy * uy + byz * uz
    qz = bxz * ux + byz * uy + bzz * uz
    square = ux * ux + uy * uy + uz * uz
    factor = 1.25 / 36.0
    base = (factor * total) * (1.0 + 1.5 * square) - (4.5 * factor) * (ux * qx + uy * qy + uz * qz)
    pull = (3.0 * factor) * total
    mx = (3.0 * factor) * ax + (9.0 * factor) * qx - pull * ux
    my = (3.0 * factor) * ay + (9.0 * factor) * qy - pull * uy
    mz = (3.0 * factor) * az + (9.0 * factor) * qz - pull * uz
    along = {
        1: mx, 3: my, 5: mz, 7: mx + my, 9: mx - my,
        11: mx + mz, 13: mx - mz, 15: my + mz, 17: my - mz,
    }
    is_solid = solid[x] > 0
    store(0, jnp.where(is_solid, h[0], base - 0.25 * h[0]))
    for k in range(1, 19, 2):
        store(k, jnp.where(is_solid, h[k + 1], (base + along[k]) - 0.25 * h[k]))
        store(k + 1, jnp.where(is_solid, h[k], (base - along[k]) - 0.25 * h[k + 1]))


def kernel(
    n_gx, n_gy, adj, pops_in, scale_in, solid_in, values_in, contact_in, cell_in,
    out_mid, out_face, out_edge, out_velocity, later, middle, pops, scale, solid, velocity, seed_values, contact, cell,
    item_out, item_in, item_all, z_hot, face_out, edge_out, edge, nothing, in_sem, out_sem, nothing_sem, item_send, item_recv, face_send, face_recv,
):
    gx, gy = lax.axis_index("gx"), lax.axis_index("gy")
    wx, wy, height = adj.shape[1:]
    cells = wx * wy

    def here(ax, ay):
        px, py = gx + ax, gy + ay
        return (px >= 0) & (px < n_gx) & (py >= 0) & (py < n_gy)

    def at(ax, ay):
        return (gx + ax, gy + ay)

    around = [(ax, ay) for ax in (-1, 0, 1) for ay in (-1, 0, 1) if (ax, ay) != (0, 0)]

    copies = {}

    def fetch(name, index, source, target):
        copies[name] = pltpu.make_async_copy(source, target, in_sem.at[index])
        copies[name].start()

    fetch("contact", 5, contact_in, contact)
    fetch("cell", 6, cell_in, cell)
    fetch("values", 7, values_in, seed_values)
    fetch("pops1", 0, pops_in.at[1], pops.at[1])
    fetch("scale", 1, scale_in, scale)
    for slot in range(19):
        pltpu.make_async_copy(adj.at[ORDER[slot]], later.at[slot, pl.ds(1, wx)], in_sem.at[2]).start()
    fetch("solid", 3, solid_in, solid)
    fetch("pops0", 4, pops_in.at[0], pops.at[0])

    barrier = pltpu.get_barrier_semaphore()
    for ax, ay in around:
        @pl.when(here(ax, ay))
        def _(ax=ax, ay=ay):
            pl.semaphore_signal(barrier, inc=1, device_id=at(ax, ay), device_id_type=MESH)

    if n_gy == 2:
        other = 1 - 2 * gy
        routes = [(ax, rel) for ax in (-1, 0, 1) for rel in (0, 1)]
        shift_of = lambda rel: rel * other
    else:
        routes = [(ax, rel) for ax in (-1, 0, 1) for rel in (-1, 0, 1)]
        shift_of = lambda rel: rel
    back = {i: routes.index((-ax, rel if n_gy == 2 else -rel)) for i, (ax, rel) in enumerate(routes)}
    for name in ("contact", "cell", "values"):
        copies[name].wait()
    count = contact.shape[1]
    per_tile = 128 // CAP
    code = contact[...]
    code_across = jnp.broadcast_to(code, (count, count))
    first = lax.broadcasted_iota(jnp.int32, (count, count), 0)
    second = lax.broadcasted_iota(jnp.int32, (count, count), 1)
    same = (code_across == code_across.T) & (first < second)
    rank = jnp.sum(same.astype(jnp.int32), axis=0, keepdims=True)
    zeros = jnp.zeros((1, count), F32)
    values = [seed_values[pop : pop + 1, :] for pop in ORDER]
    top = jnp.concatenate(values + [zeros] * 5, 0)
    top_hi = top.astype(jnp.bfloat16)
    top_lo = (top - top_hi.astype(F32)).astype(jnp.bfloat16)
    place = cell[...]
    places = jnp.concatenate(
        [(place // height).astype(F32), (place % height).astype(F32)] + [zeros] * 14, 0
    ).astype(jnp.bfloat16)
    zero_rows = jnp.zeros((8, count), jnp.bfloat16)
    table = jnp.concatenate([top_hi, zero_rows, top_lo, zero_rows, places], 0)
    for i, (ax, rel) in enumerate(routes):
        lane = rank + CAP * (back[i] % per_tile)
        wanted = (ax + 1) * 3 + shift_of(rel) + 1
        lane = jnp.where(code == wanted, lane, -1)
        choose = (first == lane).astype(F32).astype(jnp.bfloat16)
        picked = lax.dot_general(
            table, choose, (((1,), (1,)), ((), ())), preferred_element_type=F32
        )
        tile = jnp.concatenate([picked[0:24] + picked[32:56], picked[64:72]], 0)
        if (ax, rel) == (0, 0):
            item_in[back[i]] = tile
        else:
            item_out[i] = tile

    def extent(position, size):
        return 1 + (position > 0).astype(jnp.int32) + (position < size - 1).astype(jnp.int32)

    pl.semaphore_wait(barrier, extent(gx, n_gx) * extent(gy, n_gy) - 1)

    def item_copy(i):
        ax, rel = routes[i]
        return pltpu.make_async_remote_copy(
            src_ref=item_out.at[i], dst_ref=item_in.at[back[i]],
            send_sem=item_send.at[i], recv_sem=item_recv.at[back[i]],
            device_id=at(ax, shift_of(rel)), device_id_type=MESH,
        )

    for i, (ax, rel) in enumerate(routes):
        if (ax, rel) != (0, 0):
            @pl.when(here(ax, shift_of(rel)))
            def _(i=i):
                item_copy(i).start()

            @pl.when(jnp.logical_not(here(ax, shift_of(rel))))
            def _(i=i):
                item_in[i] = jnp.zeros(item_in.shape[1:], F32)

    @pl.when(jnp.logical_not(here(1, 0)))
    def _():
        later[pl.ds(0, 5), wx + 1] = jnp.zeros((5, wy, height), F32)

    @pl.when(jnp.logical_not(here(-1, 0)))
    def _():
        later[pl.ds(5, 5), 0] = jnp.zeros((5, wy, height), F32)

    corners = []
    for side, ay in ((0, 1), (1, -1)):
        for pop in Y_SETS[side]:
            if LATTICE[pop][0] != 0:
                corners.append((side, Y_SETS[side].index(pop), LATTICE[pop][0], ay))
    for side, ay in ((0, 1), (1, -1)):
        @pl.when(jnp.logical_not(here(0, ay)))
        def _(side=side):
            edge[side, :, pl.ds(8, wx), :] = jnp.zeros((5, wx, height), F32)
    for side, slot, cx, ay in corners:
        @pl.when(jnp.logical_not(here(cx, ay)))
        def _(side=side, slot=slot, cx=cx):
            edge[side, slot, pl.ds(8 + 8 * cx, 8), :] = jnp.zeros((8, height), F32)

    nothing[...] = jnp.zeros(nothing.shape, F32)
    blanks = [(out_face.at[i], nothing, cx, 0) for i, cx in enumerate((1, -1))]
    for side, ay in ((0, 1), (1, -1)):
        blanks.append((out_edge.at[side, :, pl.ds(8, wx), :], nothing.at[:, pl.ds(0, wx)], 0, ay))
    for side, slot, cx, ay in corners:
        blanks.append(
            (out_edge.at[side, slot, pl.ds(8 + 8 * cx, 8), :], nothing.at[0, pl.ds(0, 8)], cx, ay)
        )

    def blank(i):
        target, source = blanks[i][:2]
        return pltpu.make_async_copy(source, target, nothing_sem.at[i])

    for i in range(len(blanks)):
        @pl.when(jnp.logical_not(here(*blanks[i][2:])))
        def _(i=i):
            blank(i).start()

    def x_copy(stage, cx):
        pops_slot = pl.ds(0 if cx == 1 else 5, 5)
        far = wx + 1 if cx == 1 else 0
        index = 0 if cx == 1 else 1
        return pltpu.make_async_remote_copy(
            src_ref=face_out.at[stage, index],
            dst_ref=later.at[pops_slot, far] if stage == 0 else out_face.at[index],
            send_sem=face_send.at[stage, index], recv_sem=face_recv.at[stage, index],
            device_id=at(-cx, 0), device_id_type=MESH,
        )

    def y_copy(stage, side):
        target = edge if stage == 0 else out_edge
        return pltpu.make_async_remote_copy(
            src_ref=edge_out.at[stage, side], dst_ref=target.at[side, :, pl.ds(8, wx), :],
            send_sem=face_send.at[stage, 2 + side], recv_sem=face_recv.at[stage, 2 + side],
            device_id=at(0, -1 if side == 0 else 1), device_id_type=MESH,
        )

    def corner_copy(stage, number):
        side, slot, cx, ay = corners[number]
        target = edge if stage == 0 else out_edge
        return pltpu.make_async_remote_copy(
            src_ref=edge_out.at[stage, side, slot],
            dst_ref=target.at[side, slot, pl.ds(8 + 8 * cx, 8), :],
            send_sem=face_send.at[stage, 4 + number], recv_sem=face_recv.at[stage, 4 + number],
            device_id=at(-cx, -ay), device_id_type=MESH,
        )

    x_links = [(lambda stage, cx=cx: x_copy(stage, cx), cx, 0) for cx in (1, -1)]
    y_links = [(lambda stage, side=side: y_copy(stage, side), 0, 1 if side == 0 else -1) for side in (0, 1)]
    y_links += [
        (lambda stage, number=number: corner_copy(stage, number), corners[number][2], corners[number][3])
        for number in range(4)
    ]

    def start(links, stage):
        for make, cx, cy in links:
            @pl.when(here(-cx, -cy))
            def _(make=make):
                make(stage).start()

    def arrive(links, stage):
        for make, cx, cy in links:
            @pl.when(here(cx, cy))
            def _(make=make):
                make(stage).wait_recv()

    copies["pops1"].wait()
    copies["scale"].wait()

    def late(x, carry):
        velocities(pops, scale, 1, x, velocity)
        return carry

    lax.fori_loop(0, wx, late, 0)
    pltpu.make_async_copy(adj, later.at[:, pl.ds(1, wx)], in_sem.at[2]).wait()
    for side in range(2):
        line = 0 if side == 0 else wy - 1
        for index, pop in enumerate(Y_SETS[side]):
            for x in range(wx):
                edge_out[0, side, index, x : x + 1, :] = later[SLOT[pop], 1 + x, line : line + 1, :]

    for i, (ax, rel) in enumerate(routes):
        if (ax, rel) != (0, 0):
            @pl.when(here(ax, shift_of(rel)))
            def _(i=i):
                pltpu.make_async_remote_copy(
                    src_ref=item_out.at[i], dst_ref=item_in.at[i],
                    send_sem=item_send.at[i], recv_sem=item_recv.at[i],
                    device_id=at(ax, shift_of(rel)), device_id_type=MESH,
                ).wait_recv()

    tiles = -(-len(routes) // per_tile)
    wide = tiles * 128
    gathered = []
    for t in range(tiles):
        part = item_in[t * per_tile]
        for i in range(t * per_tile + 1, min((t + 1) * per_tile, len(routes))):
            part = part + item_in[i]
        gathered.append(part)
    items = jnp.concatenate(gathered, 1)
    hi = items.astype(jnp.bfloat16).astype(F32)
    item_all[0] = hi
    item_all[1] = items - hi
    for t in range(tiles):
        z_row = jnp.broadcast_to(gathered[t][25:26, :], (128, 128))
        z_of = z_row.T.astype(jnp.int32)
        for b in range(height // 128):
            lanes = lax.broadcasted_iota(jnp.int32, (128, 128), 1) + 128 * b
            z_hot[pl.ds(128 * t, 128), pl.ds(128 * b, 128)] = (
                (z_of == lanes).astype(F32).astype(jnp.bfloat16)
            )
    xy_of = items[24:25, :].astype(jnp.int32)

    def at_cells(length, first, stride):
        number = lax.broadcasted_iota(jnp.int32, (length, wide), 0)
        return number * stride + first == jnp.broadcast_to(xy_of, (length, wide))

    def field_of(rows):
        spread = jnp.concatenate(
            [
                jnp.where(match, item_all[part, slot : slot + 1, :], 0.0)
                for part in range(2)
                for slot, match in rows
            ],
            0,
        ).astype(jnp.bfloat16)
        both = jnp.dot(spread, z_hot[...], preferred_element_type=F32)
        half = both.shape[0] // 2
        return both[:half] + both[half:]

    near = [at_cells(wy, 0, 1), at_cells(wy, (wx - 1) * wy, 1)]
    line_of = [at_cells(wx, 0, wy), at_cells(wx, wy - 1, wy)]
    rows = [(5 * i + j, near[i]) for i in range(2) for j in range(5)]
    rows += [(SLOT[pop], line_of[side]) for side in range(2) for pop in Y_SETS[side]]
    outer = field_of(rows)
    for i in range(2):
        plane = later[pl.ds(5 * i, 5), 1 if i == 0 else wx]
        face_out[0, i] = plane + outer[5 * wy * i : 5 * wy * (i + 1)].reshape(5, wy, height)
    start(x_links, 0)
    begin = 10 * wy
    for side in range(2):
        part = outer[begin + 5 * wx * side : begin + 5 * wx * (side + 1)]
        edge_out[0, side] = edge_out[0, side] + part.reshape(5, wx, height)
    start(y_links, 0)

    def add_seeds(x, carry):
        match = at_cells(wy, x * wy, 1)
        seeds = field_of([(slot, match) for slot in range(19)])
        later[:, x + 1] = later[:, x + 1] + seeds.reshape(19, wy, height)
        return carry

    lax.fori_loop(0, wx, add_seeds, 0)
    copies["solid"].wait()

    def write(x):
        return pltpu.make_async_copy(middle.at[:, x], out_mid.at[:, x], out_sem.at[1 + x])

    def middle_plane(x, face=None):
        def store(pop, value):
            middle[pop, x] = value
            cx, cy = LATTICE[pop][:2]
            if cy != 0:
                side, line = (0, 0) if cy == 1 else (1, wy - 1)
                edge_out[1, side, Y_SETS[side].index(pop), pl.ds(x, 1), :] = value[line : line + 1, :]
            if face is not None and SLOT[pop] // 5 == face:
                face_out[1, face, SLOT[pop] % 5] = value

        adjoint_plane(later, SLOT, edge, velocity.at[1], solid, x, store)
        write(x).start()

    arrive(y_links, 0)
    arrive(x_links, 0)
    middle_plane(0, 0)
    middle_plane(wx - 1, 1)
    start(x_links, 1)

    def inner(x, carry):
        middle_plane(x)
        return carry

    lax.fori_loop(1, wx - 1, inner, 0)
    start(y_links, 1)

    copies["pops0"].wait()

    def early(x, carry):
        velocities(pops, scale, 0, x, velocity)
        return carry

    lax.fori_loop(0, wx, early, 0)
    velocity_write = pltpu.make_async_copy(velocity.at[0], out_velocity, out_sem.at[0])
    velocity_write.start()

    for i, (ax, rel) in enumerate(routes):
        if (ax, rel) != (0, 0):
            @pl.when(here(ax, shift_of(rel)))
            def _(i=i):
                item_copy(i).wait_send()
    for stage in range(2):
        for make, cx, cy in x_links + y_links:
            @pl.when(here(-cx, -cy))
            def _(make=make, stage=stage):
                make(stage).wait_send()
    for i in range(len(blanks)):
        @pl.when(jnp.logical_not(here(*blanks[i][2:])))
        def _(i=i):
            blank(i).wait()
    for x in range(wx):
        write(x).wait()
    velocity_write.wait()
    arrive(y_links, 1)
    arrive(x_links, 1)


def last_kernel(
    mid, face, edge_in, velocity_in, solid_in, out_init, out_mid,
    field, initial, edge, velocity, solid, side_sem, plane_sem, out_sem,
):
    wx = mid.shape[1]
    small = [
        pltpu.make_async_copy(velocity_in, velocity, side_sem.at[0]),
        pltpu.make_async_copy(solid_in, solid, side_sem.at[1]),
    ]
    for side in range(2):
        for index, pop in enumerate(Y_SETS[side]):
            cx = LATTICE[pop][0]
            span = pl.ds(0 if cx == -1 else 8, 8 if cx == 0 else 16)
            small.append(
                pltpu.make_async_copy(
                    edge_in.at[side, index, span, :], edge.at[side, index, span, :],
                    side_sem.at[2 + 5 * side + index],
                )
            )

    def face_copy(i, j):
        pop = ORDER[5 * i + j]
        return pltpu.make_async_copy(
            face.at[i, j], field.at[pop, wx + 1 if i == 0 else 0], plane_sem.at[wx + 5 * i + j]
        )

    def plane_copy(x):
        return pltpu.make_async_copy(mid.at[:, x], field.at[:, x + 1], plane_sem.at[x])

    def plane_write(x):
        return pltpu.make_async_copy(field.at[:, x + 1], out_mid.at[:, x], out_sem.at[x])

    def write(x):
        return pltpu.make_async_copy(initial.at[:, x], out_init.at[:, x], out_sem.at[wx + x])

    for j in range(5):
        face_copy(1, j).start()
    plane_copy(0).start()
    for copy in small:
        copy.start()
    for x in range(1, wx):
        plane_copy(x).start()
    for j in range(5):
        face_copy(0, j).start()

    def plane(x):
        def store(pop, value):
            initial[pop, x] = value

        adjoint_plane(field, list(range(19)), edge, velocity, solid, x, store)
        write(x).start()

    for j in range(5):
        face_copy(1, j).wait()
    plane_copy(0).wait()
    plane_write(0).start()
    for copy in small:
        copy.wait()

    def inner(x, carry):
        plane_copy(x + 1).wait()
        plane_write(x + 1).start()
        plane(x)
        return carry

    lax.fori_loop(0, wx - 1, inner, 0)
    for j in range(5):
        face_copy(0, j).wait()
    plane(wx - 1)
    for x in range(wx):
        plane_write(x).wait()
        write(x).wait()


def body(n_gx, n_gy, adj_later, saved_pops, saved_scale, solid, seed_values, seed_contact, seed_cell):
    channels, wx, wy, height = adj_later.shape
    blocks = saved_scale.shape[-1]
    count = seed_cell.shape[0]
    scale = saved_scale.transpose(0, 2, 3, 4, 1).reshape(2, wx, wy * blocks, channels)
    routes = 6 if n_gy == 2 else 9
    wide = -(-routes * CAP // 128) * 128
    field = (channels, wx, wy, height)
    in_hbm = pl.BlockSpec(memory_space=pltpu.HBM)
    shape = lambda *dims: jax.ShapeDtypeStruct(dims, F32)
    params = dict(has_side_effects=True, vmem_limit_bytes=60 * 1024 * 1024)
    mid, face, edge, velocity = pl.pallas_call(
        functools.partial(kernel, n_gx, n_gy),
        out_shape=[
            shape(*field), shape(2, 5, wy, height), shape(2, 5, wx + 16, height),
            shape(3, wx, wy, height),
        ],
        in_specs=[in_hbm] * 7,
        out_specs=[in_hbm] * 4,
        scratch_shapes=[
            pltpu.VMEM((channels, wx + 2, wy, height), F32),
            pltpu.VMEM(field, F32),
            pltpu.VMEM((2,) + field, jnp.bfloat16),
            pltpu.VMEM(scale.shape, F32),
            pltpu.VMEM((wx, wy, height), jnp.int32),
            pltpu.VMEM((2, 3, wx, wy, height), F32),
            pltpu.VMEM((channels, count), F32),
            pltpu.VMEM((1, count), jnp.int32),
            pltpu.VMEM((1, count), jnp.int32),
            pltpu.VMEM((routes, 32, 128), F32),
            pltpu.VMEM((routes, 32, 128), F32),
            pltpu.VMEM((2, 32, wide), F32),
            pltpu.VMEM((wide, height), jnp.bfloat16),
            pltpu.VMEM((2, 2, 5, wy, height), F32),
            pltpu.VMEM((2, 2, 5, wx, height), F32),
            pltpu.VMEM((2, 5, wx + 16, height), F32),
            pltpu.VMEM((5, wy, height), F32),
            pltpu.SemaphoreType.DMA((8,)),
            pltpu.SemaphoreType.DMA((1 + wx,)),
            pltpu.SemaphoreType.DMA((8,)),
            pltpu.SemaphoreType.DMA((routes,)),
            pltpu.SemaphoreType.DMA((routes,)),
            pltpu.SemaphoreType.DMA((2, 8)),
            pltpu.SemaphoreType.DMA((2, 8)),
        ],
        compiler_params=pltpu.CompilerParams(collective_id=0, **params),
    )(
        adj_later, saved_pops, scale, solid, seed_values.T,
        seed_contact.reshape(1, count), seed_cell.reshape(1, count),
    )
    return pl.pallas_call(
        last_kernel,
        out_shape=[shape(*field)] * 2,
        in_specs=[in_hbm] * 5,
        out_specs=[in_hbm] * 2,
        scratch_shapes=[
            pltpu.VMEM((channels, wx + 2, wy, height), F32),
            pltpu.VMEM(field, F32),
            pltpu.VMEM((2, 5, wx + 16, height), F32),
            pltpu.VMEM((3, wx, wy, height), F32),
            pltpu.VMEM((wx, wy, height), jnp.int32),
            pltpu.SemaphoreType.DMA((12,)),
            pltpu.SemaphoreType.DMA((wx + 10,)),
            pltpu.SemaphoreType.DMA((2 * wx,)),
        ],
        compiler_params=pltpu.CompilerParams(vmem_limit_bytes=60 * 1024 * 1024),
    )(mid, face, edge, velocity, solid)


def solution(mesh):
    n_gx, n_gy = mesh.shape["gx"], mesh.shape["gy"]
    return jax.shard_map(
        functools.partial(body, n_gx, n_gy),
        mesh=mesh,
        in_specs=(
            P(None, "gx", "gy", None),
            P(None, None, "gx", "gy", None),
            P(None, None, "gx", "gy", None),
            P("gx", "gy", None),
            P(("gx", "gy"), None),
            P(("gx", "gy"), None),
            P(("gx", "gy")),
        ),
        out_specs=(P(None, "gx", "gy", None), P(None, "gx", "gy", None)),
        check_vma=False,
    )
```

```python
import functools

import jax
import jax.numpy as jnp
from jax import lax
from jax.experimental import pallas as pl
from jax.experimental.pallas import tpu as pltpu
from jax.sharding import PartitionSpec as P

LATTICE = [
    (0, 0, 0),
    (1, 0, 0),
    (-1, 0, 0),
    (0, 1, 0),
    (0, -1, 0),
    (0, 0, 1),
    (0, 0, -1),
    (1, 1, 0),
    (-1, -1, 0),
    (1, -1, 0),
    (-1, 1, 0),
    (1, 0, 1),
    (-1, 0, -1),
    (1, 0, -1),
    (-1, 0, 1),
    (0, 1, 1),
    (0, -1, -1),
    (0, 1, -1),
    (0, -1, 1),
]
OPPOSITE = [0, 2, 1, 4, 3, 6, 5, 8, 7, 10, 9, 12, 11, 14, 13, 16, 15, 18, 17]
CAP = 32
MESH = pl.DeviceIdType.MESH
F32 = jnp.float32

ORDER = [1, 7, 9, 11, 13, 2, 8, 10, 12, 14, 0, 3, 4, 5, 6, 15, 16, 17, 18]
SLOT = [ORDER.index(pop) for pop in range(19)]
Y_SETS = [[3, 7, 10, 15, 17], [4, 8, 9, 16, 18]]


def velocities(pops, scale, step, x, out):
    rows, height = pops.shape[3], pops.shape[4]
    blocks = scale.shape[2] // rows
    length = height // blocks
    for b in range(blocks):
        span = pl.ds(b * length, length)
        factors = scale[step, x, pl.ds(b, rows, stride=blocks), :]

        def population(pop):
            stored = pops[step, pop, x, :, span].astype(F32)
            return stored * jnp.broadcast_to(factors[:, pop : pop + 1], (rows, length))

        density = population(0)
        momentum = [None, None, None]
        for k in range(1, 19, 2):
            plus, minus = population(k), population(k + 1)
            density = density + (plus + minus)
            change = plus - minus
            for axis in range(3):
                sign = LATTICE[k][axis]
                if momentum[axis] is None and sign == 1:
                    momentum[axis] = change
                elif sign == 1:
                    momentum[axis] = momentum[axis] + change
                elif sign == -1:
                    momentum[axis] = momentum[axis] - change
        inverse = 1.0 / density
        for axis in range(3):
            out[step, axis, x, :, span] = momentum[axis] * inverse


def adjoint_plane(field, slots, edge, velocity, solid, x, store):
    rows, height = field.shape[2], field.shape[3]
    for r in range(rows // 8):
        for c in range(height // 128):
            adjoint_tile(field, slots, edge, velocity, solid, x, r, c, store)


def adjoint_tile(field, slots, edge, velocity, solid, x, r, c, store):
    rows, height = field.shape[2], field.shape[3]
    row = lax.broadcasted_iota(jnp.int32, (8, 128), 0)
    col = lax.broadcasted_iota(jnp.int32, (8, 128), 1)

    def along_y(pop, c):
        cx, cy = LATTICE[pop][:2]
        span = pl.ds(c * 128, 128)
        value = field[slots[pop], x + 1 + cx, pl.ds(r * 8, 8), span]
        if cy == 0:
            return value
        beyond = r * 8 + (8 if cy == 1 else -1)
        if 0 <= beyond < rows:
            line = field[slots[pop], x + 1 + cx, pl.ds(beyond, 1), span]
        else:
            side = 0 if cy == 1 else 1
            line = edge[side, Y_SETS[side].index(pop), pl.ds(x + cx + 8, 1), :]
            line = line[:, c * 128 : (c + 1) * 128]
        turned = pltpu.roll(value, 7 if cy == 1 else 1, 0)
        return jnp.where(row == (7 if cy == 1 else 0), jnp.broadcast_to(line, (8, 128)), turned)

    def moved(pop):
        cz = LATTICE[pop][2]
        value = along_y(pop, c)
        if cz == 0:
            return value
        shift = 127 if cz == 1 else 1
        beyond = 0.0
        if 0 <= c + cz < height // 128:
            beyond = pltpu.roll(along_y(pop, c + cz), shift, 1)
        return jnp.where(col == (127 if cz == 1 else 0), beyond, pltpu.roll(value, shift, 1))

    h = [moved(pop) for pop in range(19)]
    s = {k: h[k] + h[k + 1] for k in range(1, 19, 2)}
    d = {k: h[k] - h[k + 1] for k in range(1, 19, 2)}
    diagonal = s[7] + s[9] + s[11] + s[13] + s[15] + s[17]
    total = 12.0 * h[0] + 2.0 * (s[1] + s[3] + s[5]) + diagonal
    ax = 2.0 * d[1] + d[7] + d[9] + d[11] + d[13]
    ay = 2.0 * d[3] + d[7] - d[9] + d[15] + d[17]
    az = 2.0 * d[5] + d[11] - d[13] + d[15] - d[17]
    bxx = 2.0 * s[1] + (s[7] + s[9]) + (s[11] + s[13])
    byy = 2.0 * s[3] + (s[7] + s[9]) + (s[15] + s[17])
    bzz = 2.0 * s[5] + (s[11] + s[13]) + (s[15] + s[17])
    bxy, bxz, byz = s[7] - s[9], s[11] - s[13], s[15] - s[17]
    here = (pl.ds(r * 8, 8), pl.ds(c * 128, 128))
    ux, uy, uz = [velocity[(axis, x) + here] for axis in range(3)]
    qx = bxx * ux + bxy * uy + bxz * uz
    qy = bxy * ux + byy * uy + byz * uz
    qz = bxz * ux + byz * uy + bzz * uz
    square = ux * ux + uy * uy + uz * uz
    factor = 1.25 / 36.0
    base = (factor * total) * (1.0 + 1.5 * square) - (4.5 * factor) * (ux * qx + uy * qy + uz * qz)
    pull = (3.0 * factor) * total
    mx = (3.0 * factor) * ax + (9.0 * factor) * qx - pull * ux
    my = (3.0 * factor) * ay + (9.0 * factor) * qy - pull * uy
    mz = (3.0 * factor) * az + (9.0 * factor) * qz - pull * uz
    along = {
        1: mx, 3: my, 5: mz, 7: mx + my, 9: mx - my,
        11: mx + mz, 13: mx - mz, 15: my + mz, 17: my - mz,
    }
    is_solid = solid[(x,) + here] > 0
    store(0, r, c, jnp.where(is_solid, h[0], base - 0.25 * h[0]))
    for k in range(1, 19, 2):
        store(k, r, c, jnp.where(is_solid, h[k + 1], (base + along[k]) - 0.25 * h[k]))
        store(k + 1, r, c, jnp.where(is_solid, h[k], (base - along[k]) - 0.25 * h[k + 1]))


def kernel(
    n_gx, n_gy, adj, pops_in, scale_in, solid_in, values_in, contact_in, cell_in,
    out_mid, out_face, out_edge, out_velocity, later, middle, pops, scale, solid, velocity, seed_values, contact, cell,
    item_out, item_in, item_all, z_hot, face_out, edge_out, edge, nothing, in_sem, out_sem, nothing_sem, item_send, item_recv, face_send, face_recv,
):
    gx, gy = lax.axis_index("gx"), lax.axis_index("gy")
    wx, wy, height = adj.shape[1:]
    cells = wx * wy

    def here(ax, ay):
        px, py = gx + ax, gy + ay
        return (px >= 0) & (px < n_gx) & (py >= 0) & (py < n_gy)

    def at(ax, ay):
        return (gx + ax, gy + ay)

    around = [(ax, ay) for ax in (-1, 0, 1) for ay in (-1, 0, 1) if (ax, ay) != (0, 0)]

    copies = {}

    def fetch(name, index, source, target):
        copies[name] = pltpu.make_async_copy(source, target, in_sem.at[index])
        copies[name].start()

    fetch("contact", 5, contact_in, contact)
    fetch("cell", 6, cell_in, cell)
    fetch("values", 7, values_in, seed_values)
    fetch("pops1", 0, pops_in.at[1], pops.at[1])
    fetch("scale", 1, scale_in, scale)
    for slot in range(19):
        pltpu.make_async_copy(adj.at[ORDER[slot]], later.at[slot, pl.ds(1, wx)], in_sem.at[2]).start()
    fetch("solid", 3, solid_in, solid)
    fetch("pops0", 4, pops_in.at[0], pops.at[0])

    barrier = pltpu.get_barrier_semaphore()
    for ax, ay in around:
        @pl.when(here(ax, ay))
        def _(ax=ax, ay=ay):
            pl.semaphore_signal(barrier, inc=1, device_id=at(ax, ay), device_id_type=MESH)

    if n_gy == 2:
        other = 1 - 2 * gy
        routes = [(ax, rel) for ax in (-1, 0, 1) for rel in (0, 1)]
        shift_of = lambda rel: rel * other
    else:
        routes = [(ax, rel) for ax in (-1, 0, 1) for rel in (-1, 0, 1)]
        shift_of = lambda rel: rel
    back = {i: routes.index((-ax, rel if n_gy == 2 else -rel)) for i, (ax, rel) in enumerate(routes)}
    for name in ("contact", "cell", "values"):
        copies[name].wait()
    count = contact.shape[1]
    per_tile = 128 // CAP
    code = contact[...]
    code_across = jnp.broadcast_to(code, (count, count))
    first = lax.broadcasted_iota(jnp.int32, (count, count), 0)
    second = lax.broadcasted_iota(jnp.int32, (count, count), 1)
    same = (code_across == code_across.T) & (first < second)
    rank = jnp.sum(same.astype(jnp.int32), axis=0, keepdims=True)
    zeros = jnp.zeros((1, count), F32)
    values = [seed_values[pop : pop + 1, :] for pop in ORDER]
    top = jnp.concatenate(values + [zeros] * 5, 0)
    top_hi = top.astype(jnp.bfloat16)
    top_lo = (top - top_hi.astype(F32)).astype(jnp.bfloat16)
    place = cell[...]
    places = jnp.concatenate(
        [(place // height).astype(F32), (place % height).astype(F32)] + [zeros] * 14, 0
    ).astype(jnp.bfloat16)
    zero_rows = jnp.zeros((8, count), jnp.bfloat16)
    table = jnp.concatenate([top_hi, zero_rows, top_lo, zero_rows, places], 0)
    for i, (ax, rel) in enumerate(routes):
        lane = rank + CAP * (back[i] % per_tile)
        wanted = (ax + 1) * 3 + shift_of(rel) + 1
        lane = jnp.where(code == wanted, lane, -1)
        choose = (first == lane).astype(F32).astype(jnp.bfloat16)
        picked = lax.dot_general(
            table, choose, (((1,), (1,)), ((), ())), preferred_element_type=F32
        )
        tile = jnp.concatenate([picked[0:24] + picked[32:56], picked[64:72]], 0)
        if (ax, rel) == (0, 0):
            item_in[back[i]] = tile
        else:
            item_out[i] = tile

    def extent(position, size):
        return 1 + (position > 0).astype(jnp.int32) + (position < size - 1).astype(jnp.int32)

    pl.semaphore_wait(barrier, extent(gx, n_gx) * extent(gy, n_gy) - 1)

    def item_copy(i):
        ax, rel = routes[i]
        return pltpu.make_async_remote_copy(
            src_ref=item_out.at[i], dst_ref=item_in.at[back[i]],
            send_sem=item_send.at[i], recv_sem=item_recv.at[back[i]],
            device_id=at(ax, shift_of(rel)), device_id_type=MESH,
        )

    for i, (ax, rel) in enumerate(routes):
        if (ax, rel) != (0, 0):
            @pl.when(here(ax, shift_of(rel)))
            def _(i=i):
                item_copy(i).start()

            @pl.when(jnp.logical_not(here(ax, shift_of(rel))))
            def _(i=i):
                item_in[i] = jnp.zeros(item_in.shape[1:], F32)

    @pl.when(jnp.logical_not(here(1, 0)))
    def _():
        later[pl.ds(0, 5), wx + 1] = jnp.zeros((5, wy, height), F32)

    @pl.when(jnp.logical_not(here(-1, 0)))
    def _():
        later[pl.ds(5, 5), 0] = jnp.zeros((5, wy, height), F32)

    corners = []
    for side, ay in ((0, 1), (1, -1)):
        for pop in Y_SETS[side]:
            if LATTICE[pop][0] != 0:
                corners.append((side, Y_SETS[side].index(pop), LATTICE[pop][0], ay))
    for side, ay in ((0, 1), (1, -1)):
        @pl.when(jnp.logical_not(here(0, ay)))
        def _(side=side):
            edge[side, :, pl.ds(8, wx), :] = jnp.zeros((5, wx, height), F32)
    for side, slot, cx, ay in corners:
        @pl.when(jnp.logical_not(here(cx, ay)))
        def _(side=side, slot=slot, cx=cx):
            edge[side, slot, pl.ds(8 + 8 * cx, 8), :] = jnp.zeros((8, height), F32)

    nothing[...] = jnp.zeros(nothing.shape, F32)
    blanks = [(out_face.at[i], nothing, cx, 0) for i, cx in enumerate((1, -1))]
    for side, ay in ((0, 1), (1, -1)):
        blanks.append((out_edge.at[side, :, pl.ds(8, wx), :], nothing.at[:, pl.ds(0, wx)], 0, ay))
    for side, slot, cx, ay in corners:
        blanks.append(
            (out_edge.at[side, slot, pl.ds(8 + 8 * cx, 8), :], nothing.at[0, pl.ds(0, 8)], cx, ay)
        )

    def blank(i):
        target, source = blanks[i][:2]
        return pltpu.make_async_copy(source, target, nothing_sem.at[i])

    for i in range(len(blanks)):
        @pl.when(jnp.logical_not(here(*blanks[i][2:])))
        def _(i=i):
            blank(i).start()

    def x_copy(stage, cx):
        pops_slot = pl.ds(0 if cx == 1 else 5, 5)
        far = wx + 1 if cx == 1 else 0
        index = 0 if cx == 1 else 1
        return pltpu.make_async_remote_copy(
            src_ref=face_out.at[stage, index],
            dst_ref=later.at[pops_slot, far] if stage == 0 else out_face.at[index],
            send_sem=face_send.at[stage, index], recv_sem=face_recv.at[stage, index],
            device_id=at(-cx, 0), device_id_type=MESH,
        )

    def y_copy(stage, side):
        target = edge if stage == 0 else out_edge
        return pltpu.make_async_remote_copy(
            src_ref=edge_out.at[stage, side], dst_ref=target.at[side, :, pl.ds(8, wx), :],
            send_sem=face_send.at[stage, 2 + side], recv_sem=face_recv.at[stage, 2 + side],
            device_id=at(0, -1 if side == 0 else 1), device_id_type=MESH,
        )

    def corner_copy(stage, number):
        side, slot, cx, ay = corners[number]
        target = edge if stage == 0 else out_edge
        return pltpu.make_async_remote_copy(
            src_ref=edge_out.at[stage, side, slot],
            dst_ref=target.at[side, slot, pl.ds(8 + 8 * cx, 8), :],
            send_sem=face_send.at[stage, 4 + number], recv_sem=face_recv.at[stage, 4 + number],
            device_id=at(-cx, -ay), device_id_type=MESH,
        )

    x_links = [(lambda stage, cx=cx: x_copy(stage, cx), cx, 0) for cx in (1, -1)]
    y_links = [(lambda stage, side=side: y_copy(stage, side), 0, 1 if side == 0 else -1) for side in (0, 1)]
    y_links += [
        (lambda stage, number=number: corner_copy(stage, number), corners[number][2], corners[number][3])
        for number in range(4)
    ]

    def start(links, stage):
        for make, cx, cy in links:
            @pl.when(here(-cx, -cy))
            def _(make=make):
                make(stage).start()

    def arrive(links, stage):
        for make, cx, cy in links:
            @pl.when(here(cx, cy))
            def _(make=make):
                make(stage).wait_recv()

    copies["pops1"].wait()
    copies["scale"].wait()

    def late(x, carry):
        velocities(pops, scale, 1, x, velocity)
        return carry

    lax.fori_loop(0, wx, late, 0)
    pltpu.make_async_copy(adj, later.at[:, pl.ds(1, wx)], in_sem.at[2]).wait()
    for side in range(2):
        line = 0 if side == 0 else wy - 1
        for index, pop in enumerate(Y_SETS[side]):
            for x in range(wx):
                edge_out[0, side, index, x : x + 1, :] = later[SLOT[pop], 1 + x, line : line + 1, :]

    for i, (ax, rel) in enumerate(routes):
        if (ax, rel) != (0, 0):
            @pl.when(here(ax, shift_of(rel)))
            def _(i=i):
                pltpu.make_async_remote_copy(
                    src_ref=item_out.at[i], dst_ref=item_in.at[i],
                    send_sem=item_send.at[i], recv_sem=item_recv.at[i],
                    device_id=at(ax, shift_of(rel)), device_id_type=MESH,
                ).wait_recv()

    tiles = -(-len(routes) // per_tile)
    wide = tiles * 128
    gathered = []
    for t in range(tiles):
        part = item_in[t * per_tile]
        for i in range(t * per_tile + 1, min((t + 1) * per_tile, len(routes))):
            part = part + item_in[i]
        gathered.append(part)
    items = jnp.concatenate(gathered, 1)
    hi = items.astype(jnp.bfloat16).astype(F32)
    item_all[0] = hi
    item_all[1] = items - hi
    for t in range(tiles):
        z_row = jnp.broadcast_to(gathered[t][25:26, :], (128, 128))
        z_of = z_row.T.astype(jnp.int32)
        for b in range(height // 128):
            lanes = lax.broadcasted_iota(jnp.int32, (128, 128), 1) + 128 * b
            z_hot[pl.ds(128 * t, 128), pl.ds(128 * b, 128)] = (
                (z_of == lanes).astype(F32).astype(jnp.bfloat16)
            )
    xy_of = items[24:25, :].astype(jnp.int32)

    def at_cells(length, first, stride):
        number = lax.broadcasted_iota(jnp.int32, (length, wide), 0)
        return number * stride + first == jnp.broadcast_to(xy_of, (length, wide))

    def field_of(rows):
        spread = jnp.concatenate(
            [
                jnp.where(match, item_all[part, slot : slot + 1, :], 0.0)
                for part in range(2)
                for slot, match in rows
            ],
            0,
        ).astype(jnp.bfloat16)
        both = jnp.dot(spread, z_hot[...], preferred_element_type=F32)
        half = both.shape[0] // 2
        return both[:half] + both[half:]

    near = [at_cells(wy, 0, 1), at_cells(wy, (wx - 1) * wy, 1)]
    line_of = [at_cells(wx, 0, wy), at_cells(wx, wy - 1, wy)]
    rows = [(5 * i + j, near[i]) for i in range(2) for j in range(5)]
    rows += [(SLOT[pop], line_of[side]) for side in range(2) for pop in Y_SETS[side]]
    outer = field_of(rows)
    for i in range(2):
        plane = later[pl.ds(5 * i, 5), 1 if i == 0 else wx]
        face_out[0, i] = plane + outer[5 * wy * i : 5 * wy * (i + 1)].reshape(5, wy, height)
    start(x_links, 0)
    begin = 10 * wy
    for side in range(2):
        part = outer[begin + 5 * wx * side : begin + 5 * wx * (side + 1)]
        edge_out[0, side] = edge_out[0, side] + part.reshape(5, wx, height)
    start(y_links, 0)

    def add_seeds(x, carry):
        match = at_cells(wy, x * wy, 1)
        seeds = field_of([(slot, match) for slot in range(19)])
        later[:, x + 1] = later[:, x + 1] + seeds.reshape(19, wy, height)
        return carry

    lax.fori_loop(0, wx, add_seeds, 0)
    copies["solid"].wait()

    def write(x):
        return pltpu.make_async_copy(middle.at[:, x], out_mid.at[:, x], out_sem.at[1 + x])

    def middle_plane(x, face=None):
        lines = {}

        def store(pop, r, c, value):
            span = pl.ds(c * 128, 128)
            middle[pop, x, pl.ds(r * 8, 8), span] = value
            cx, cy = LATTICE[pop][:2]
            if (cy == 1 and r == 0) or (cy == -1 and r == wy // 8 - 1):
                side, line = (0, 0) if cy == 1 else (1, 7)
                lines.setdefault(pop, []).append(value[line : line + 1])
                if c == height // 128 - 1:
                    whole = jnp.concatenate(lines[pop], 1)
                    edge_out[1, side, Y_SETS[side].index(pop), pl.ds(x, 1), :] = whole
            if face is not None and SLOT[pop] // 5 == face:
                face_out[1, face, SLOT[pop] % 5, pl.ds(r * 8, 8), span] = value

        adjoint_plane(later, SLOT, edge, velocity.at[1], solid, x, store)
        write(x).start()

    arrive(y_links, 0)
    arrive(x_links, 0)
    middle_plane(0, 0)
    middle_plane(wx - 1, 1)
    start(x_links, 1)

    def inner(x, carry):
        middle_plane(x)
        return carry

    lax.fori_loop(1, wx - 1, inner, 0)
    start(y_links, 1)

    copies["pops0"].wait()

    def early(x, carry):
        velocities(pops, scale, 0, x, velocity)
        return carry

    lax.fori_loop(0, wx, early, 0)
    velocity_write = pltpu.make_async_copy(velocity.at[0], out_velocity, out_sem.at[0])
    velocity_write.start()

    for i, (ax, rel) in enumerate(routes):
        if (ax, rel) != (0, 0):
            @pl.when(here(ax, shift_of(rel)))
            def _(i=i):
                item_copy(i).wait_send()
    for stage in range(2):
        for make, cx, cy in x_links + y_links:
            @pl.when(here(-cx, -cy))
            def _(make=make, stage=stage):
                make(stage).wait_send()
    for i in range(len(blanks)):
        @pl.when(jnp.logical_not(here(*blanks[i][2:])))
        def _(i=i):
            blank(i).wait()
    for x in range(wx):
        write(x).wait()
    velocity_write.wait()
    arrive(y_links, 1)
    arrive(x_links, 1)


def last_kernel(
    mid, face, edge_in, velocity_in, solid_in, out_init, out_mid,
    field, initial, edge, velocity, solid, side_sem, plane_sem, out_sem,
):
    wx = mid.shape[1]
    small = [
        pltpu.make_async_copy(velocity_in, velocity, side_sem.at[0]),
        pltpu.make_async_copy(solid_in, solid, side_sem.at[1]),
    ]
    for side in range(2):
        for index, pop in enumerate(Y_SETS[side]):
            cx = LATTICE[pop][0]
            span = pl.ds(0 if cx == -1 else 8, 8 if cx == 0 else 16)
            small.append(
                pltpu.make_async_copy(
                    edge_in.at[side, index, span, :], edge.at[side, index, span, :],
                    side_sem.at[2 + 5 * side + index],
                )
            )

    def face_copy(i, j):
        pop = ORDER[5 * i + j]
        return pltpu.make_async_copy(
            face.at[i, j], field.at[pop, wx + 1 if i == 0 else 0], plane_sem.at[wx + 5 * i + j]
        )

    def plane_copy(x):
        return pltpu.make_async_copy(mid.at[:, x], field.at[:, x + 1], plane_sem.at[x])

    def plane_write(x):
        return pltpu.make_async_copy(field.at[:, x + 1], out_mid.at[:, x], out_sem.at[x])

    def write(x):
        return pltpu.make_async_copy(initial.at[:, x], out_init.at[:, x], out_sem.at[wx + x])

    for j in range(5):
        face_copy(1, j).start()
    plane_copy(0).start()
    for copy in small:
        copy.start()
    for x in range(1, wx):
        plane_copy(x).start()
    for j in range(5):
        face_copy(0, j).start()

    def plane(x):
        def store(pop, r, c, value):
            initial[pop, x, pl.ds(r * 8, 8), pl.ds(c * 128, 128)] = value

        adjoint_plane(field, list(range(19)), edge, velocity, solid, x, store)
        write(x).start()

    for j in range(5):
        face_copy(1, j).wait()
    plane_copy(0).wait()
    plane_write(0).start()
    for copy in small:
        copy.wait()

    def inner(x, carry):
        plane_copy(x + 1).wait()
        plane_write(x + 1).start()
        plane(x)
        return carry

    lax.fori_loop(0, wx - 1, inner, 0)
    for j in range(5):
        face_copy(0, j).wait()
    plane(wx - 1)
    for x in range(wx):
        plane_write(x).wait()
        write(x).wait()


def body(n_gx, n_gy, adj_later, saved_pops, saved_scale, solid, seed_values, seed_contact, seed_cell):
    channels, wx, wy, height = adj_later.shape
    blocks = saved_scale.shape[-1]
    count = seed_cell.shape[0]
    scale = saved_scale.transpose(0, 2, 3, 4, 1).reshape(2, wx, wy * blocks, channels)
    routes = 6 if n_gy == 2 else 9
    wide = -(-routes * CAP // 128) * 128
    field = (channels, wx, wy, height)
    in_hbm = pl.BlockSpec(memory_space=pltpu.HBM)
    shape = lambda *dims: jax.ShapeDtypeStruct(dims, F32)
    params = dict(has_side_effects=True, vmem_limit_bytes=60 * 1024 * 1024)
    mid, face, edge, velocity = pl.pallas_call(
        functools.partial(kernel, n_gx, n_gy),
        out_shape=[
            shape(*field), shape(2, 5, wy, height), shape(2, 5, wx + 16, height),
            shape(3, wx, wy, height),
        ],
        in_specs=[in_hbm] * 7,
        out_specs=[in_hbm] * 4,
        scratch_shapes=[
            pltpu.VMEM((channels, wx + 2, wy, height), F32),
            pltpu.VMEM(field, F32),
            pltpu.VMEM((2,) + field, jnp.bfloat16),
            pltpu.VMEM(scale.shape, F32),
            pltpu.VMEM((wx, wy, height), jnp.int32),
            pltpu.VMEM((2, 3, wx, wy, height), F32),
            pltpu.VMEM((channels, count), F32),
            pltpu.VMEM((1, count), jnp.int32),
            pltpu.VMEM((1, count), jnp.int32),
            pltpu.VMEM((routes, 32, 128), F32),
            pltpu.VMEM((routes, 32, 128), F32),
            pltpu.VMEM((2, 32, wide), F32),
            pltpu.VMEM((wide, height), jnp.bfloat16),
            pltpu.VMEM((2, 2, 5, wy, height), F32),
            pltpu.VMEM((2, 2, 5, wx, height), F32),
            pltpu.VMEM((2, 5, wx + 16, height), F32),
            pltpu.VMEM((5, wy, height), F32),
            pltpu.SemaphoreType.DMA((8,)),
            pltpu.SemaphoreType.DMA((1 + wx,)),
            pltpu.SemaphoreType.DMA((8,)),
            pltpu.SemaphoreType.DMA((routes,)),
            pltpu.SemaphoreType.DMA((routes,)),
            pltpu.SemaphoreType.DMA((2, 8)),
            pltpu.SemaphoreType.DMA((2, 8)),
        ],
        compiler_params=pltpu.CompilerParams(collective_id=0, **params),
    )(
        adj_later, saved_pops, scale, solid, seed_values.T,
        seed_contact.reshape(1, count), seed_cell.reshape(1, count),
    )
    return pl.pallas_call(
        last_kernel,
        out_shape=[shape(*field)] * 2,
        in_specs=[in_hbm] * 5,
        out_specs=[in_hbm] * 2,
        scratch_shapes=[
            pltpu.VMEM((channels, wx + 2, wy, height), F32),
            pltpu.VMEM(field, F32),
            pltpu.VMEM((2, 5, wx + 16, height), F32),
            pltpu.VMEM((3, wx, wy, height), F32),
            pltpu.VMEM((wx, wy, height), jnp.int32),
            pltpu.SemaphoreType.DMA((12,)),
            pltpu.SemaphoreType.DMA((wx + 10,)),
            pltpu.SemaphoreType.DMA((2 * wx,)),
        ],
        compiler_params=pltpu.CompilerParams(vmem_limit_bytes=60 * 1024 * 1024),
    )(mid, face, edge, velocity, solid)


def solution(mesh):
    n_gx, n_gy = mesh.shape["gx"], mesh.shape["gy"]
    return jax.shard_map(
        functools.partial(body, n_gx, n_gy),
        mesh=mesh,
        in_specs=(
            P(None, "gx", "gy", None),
            P(None, None, "gx", "gy", None),
            P(None, None, "gx", "gy", None),
            P("gx", "gy", None),
            P(("gx", "gy"), None),
            P(("gx", "gy"), None),
            P(("gx", "gy")),
        ),
        out_specs=(P(None, "gx", "gy", None), P(None, "gx", "gy", None)),
        check_vma=False,
    )
```

```python
import functools

import jax
import jax.numpy as jnp
from jax import lax
from jax.experimental import pallas as pl
from jax.experimental.pallas import tpu as pltpu
from jax.sharding import PartitionSpec as P

LATTICE = [
    (0, 0, 0),
    (1, 0, 0),
    (-1, 0, 0),
    (0, 1, 0),
    (0, -1, 0),
    (0, 0, 1),
    (0, 0, -1),
    (1, 1, 0),
    (-1, -1, 0),
    (1, -1, 0),
    (-1, 1, 0),
    (1, 0, 1),
    (-1, 0, -1),
    (1, 0, -1),
    (-1, 0, 1),
    (0, 1, 1),
    (0, -1, -1),
    (0, 1, -1),
    (0, -1, 1),
]
OPPOSITE = [0, 2, 1, 4, 3, 6, 5, 8, 7, 10, 9, 12, 11, 14, 13, 16, 15, 18, 17]
CAP = 32
MESH = pl.DeviceIdType.MESH
F32 = jnp.float32

ORDER = [1, 7, 9, 11, 13, 2, 8, 10, 12, 14, 0, 3, 4, 5, 6, 15, 16, 17, 18]
SLOT = [ORDER.index(pop) for pop in range(19)]
Y_SETS = [[3, 7, 10, 15, 17], [4, 8, 9, 16, 18]]


def velocities(pops, scale, step, x, out):
    rows, height = pops.shape[3], pops.shape[4]
    blocks = scale.shape[2] // rows
    length = height // blocks
    for b in range(blocks):
        span = pl.ds(b * length, length)
        factors = scale[step, x, pl.ds(b, rows, stride=blocks), :]

        def population(pop):
            stored = pops[step, pop, x, :, span].astype(F32)
            return stored * jnp.broadcast_to(factors[:, pop : pop + 1], (rows, length))

        density = population(0)
        momentum = [None, None, None]
        for k in range(1, 19, 2):
            plus, minus = population(k), population(k + 1)
            density = density + (plus + minus)
            change = plus - minus
            for axis in range(3):
                sign = LATTICE[k][axis]
                if momentum[axis] is None and sign == 1:
                    momentum[axis] = change
                elif sign == 1:
                    momentum[axis] = momentum[axis] + change
                elif sign == -1:
                    momentum[axis] = momentum[axis] - change
        inverse = 1.0 / density
        for axis in range(3):
            out[step, axis, x, :, span] = momentum[axis] * inverse


def adjoint_plane(field, slots, edge, velocity, solid, x, store):
    rows, height = field.shape[2], field.shape[3]
    for r in range(rows // 8):
        for c in range(height // 128):
            adjoint_tile(field, slots, edge, velocity, solid, x, r, c, store)


def adjoint_tile(field, slots, edge, velocity, solid, x, r, c, store):
    rows, height = field.shape[2], field.shape[3]
    row = lax.broadcasted_iota(jnp.int32, (8, 128), 0)
    col = lax.broadcasted_iota(jnp.int32, (8, 128), 1)

    def along_y(pop, c):
        cx, cy = LATTICE[pop][:2]
        span = pl.ds(c * 128, 128)
        value = field[slots[pop], x + 1 + cx, pl.ds(r * 8, 8), span]
        if cy == 0:
            return value
        beyond = r * 8 + (8 if cy == 1 else -1)
        if 0 <= beyond < rows:
            line = field[slots[pop], x + 1 + cx, pl.ds(beyond, 1), span]
        else:
            side = 0 if cy == 1 else 1
            line = edge[side, Y_SETS[side].index(pop), pl.ds(x + cx + 8, 1), :]
            line = line[:, c * 128 : (c + 1) * 128]
        turned = pltpu.roll(value, 7 if cy == 1 else 1, 0)
        return jnp.where(row == (7 if cy == 1 else 0), jnp.broadcast_to(line, (8, 128)), turned)

    def moved(pop):
        cz = LATTICE[pop][2]
        value = along_y(pop, c)
        if cz == 0:
            return value
        shift = 127 if cz == 1 else 1
        beyond = 0.0
        if 0 <= c + cz < height // 128:
            beyond = pltpu.roll(along_y(pop, c + cz), shift, 1)
        return jnp.where(col == (127 if cz == 1 else 0), beyond, pltpu.roll(value, shift, 1))

    h = [moved(pop) for pop in range(19)]
    s = {k: h[k] + h[k + 1] for k in range(1, 19, 2)}
    d = {k: h[k] - h[k + 1] for k in range(1, 19, 2)}
    diagonal = s[7] + s[9] + s[11] + s[13] + s[15] + s[17]
    total = 12.0 * h[0] + 2.0 * (s[1] + s[3] + s[5]) + diagonal
    ax = 2.0 * d[1] + d[7] + d[9] + d[11] + d[13]
    ay = 2.0 * d[3] + d[7] - d[9] + d[15] + d[17]
    az = 2.0 * d[5] + d[11] - d[13] + d[15] - d[17]
    bxx = 2.0 * s[1] + (s[7] + s[9]) + (s[11] + s[13])
    byy = 2.0 * s[3] + (s[7] + s[9]) + (s[15] + s[17])
    bzz = 2.0 * s[5] + (s[11] + s[13]) + (s[15] + s[17])
    bxy, bxz, byz = s[7] - s[9], s[11] - s[13], s[15] - s[17]
    here = (pl.ds(r * 8, 8), pl.ds(c * 128, 128))
    ux, uy, uz = [velocity[(axis, x) + here] for axis in range(3)]
    qx = bxx * ux + bxy * uy + bxz * uz
    qy = bxy * ux + byy * uy + byz * uz
    qz = bxz * ux + byz * uy + bzz * uz
    square = ux * ux + uy * uy + uz * uz
    factor = 1.25 / 36.0
    base = (factor * total) * (1.0 + 1.5 * square) - (4.5 * factor) * (ux * qx + uy * qy + uz * qz)
    pull = (3.0 * factor) * total
    mx = (3.0 * factor) * ax + (9.0 * factor) * qx - pull * ux
    my = (3.0 * factor) * ay + (9.0 * factor) * qy - pull * uy
    mz = (3.0 * factor) * az + (9.0 * factor) * qz - pull * uz
    along = {
        1: mx, 3: my, 5: mz, 7: mx + my, 9: mx - my,
        11: mx + mz, 13: mx - mz, 15: my + mz, 17: my - mz,
    }
    is_solid = solid[(x,) + here] > 0
    store(0, r, c, jnp.where(is_solid, h[0], base - 0.25 * h[0]))
    for k in range(1, 19, 2):
        store(k, r, c, jnp.where(is_solid, h[k + 1], (base + along[k]) - 0.25 * h[k]))
        store(k + 1, r, c, jnp.where(is_solid, h[k], (base - along[k]) - 0.25 * h[k + 1]))


def kernel(
    n_gx, n_gy, adj, pops_in, scale_in, solid_in, values_in, contact_in, cell_in,
    out_mid, out_face, out_edge, out_velocity, later, middle, pops, scale, solid, velocity, seed_values, contact, cell,
    item_out, item_in, item_all, z_hot, face_out, edge_out, edge, nothing, in_sem, out_sem, nothing_sem, item_send, item_recv, face_send, face_recv,
):
    gx, gy = lax.axis_index("gx"), lax.axis_index("gy")
    wx, wy, height = adj.shape[1:]
    cells = wx * wy

    def here(ax, ay):
        px, py = gx + ax, gy + ay
        return (px >= 0) & (px < n_gx) & (py >= 0) & (py < n_gy)

    def at(ax, ay):
        return (gx + ax, gy + ay)

    around = [(ax, ay) for ax in (-1, 0, 1) for ay in (-1, 0, 1) if (ax, ay) != (0, 0)]

    copies = {}

    def fetch(name, index, source, target):
        copies[name] = pltpu.make_async_copy(source, target, in_sem.at[index])
        copies[name].start()

    fetch("contact", 5, contact_in, contact)
    fetch("cell", 6, cell_in, cell)
    fetch("values", 7, values_in, seed_values)
    fetch("pops1", 0, pops_in.at[1], pops.at[1])
    fetch("scale", 1, scale_in, scale)
    for slot in range(19):
        pltpu.make_async_copy(adj.at[ORDER[slot]], later.at[slot, pl.ds(1, wx)], in_sem.at[2]).start()
    fetch("solid", 3, solid_in, solid)
    fetch("pops0", 4, pops_in.at[0], pops.at[0])

    barrier = pltpu.get_barrier_semaphore()
    for ax, ay in around:
        @pl.when(here(ax, ay))
        def _(ax=ax, ay=ay):
            pl.semaphore_signal(barrier, inc=1, device_id=at(ax, ay), device_id_type=MESH)

    if n_gy == 2:
        other = 1 - 2 * gy
        routes = [(ax, rel) for ax in (-1, 0, 1) for rel in (0, 1)]
        shift_of = lambda rel: rel * other
    else:
        routes = [(ax, rel) for ax in (-1, 0, 1) for rel in (-1, 0, 1)]
        shift_of = lambda rel: rel
    back = {i: routes.index((-ax, rel if n_gy == 2 else -rel)) for i, (ax, rel) in enumerate(routes)}
    for name in ("contact", "cell", "values"):
        copies[name].wait()
    count = contact.shape[1]
    per_tile = 128 // CAP
    code = contact[...]
    code_across = jnp.broadcast_to(code, (count, count))
    first = lax.broadcasted_iota(jnp.int32, (count, count), 0)
    second = lax.broadcasted_iota(jnp.int32, (count, count), 1)
    same = (code_across == code_across.T) & (first < second)
    rank = jnp.sum(same.astype(jnp.int32), axis=0, keepdims=True)
    zeros = jnp.zeros((1, count), F32)
    values = [seed_values[pop : pop + 1, :] for pop in ORDER]
    top = jnp.concatenate(values + [zeros] * 5, 0)
    top_hi = top.astype(jnp.bfloat16)
    top_lo = (top - top_hi.astype(F32)).astype(jnp.bfloat16)
    place = cell[...]
    places = jnp.concatenate(
        [(place // height).astype(F32), (place % height).astype(F32)] + [zeros] * 14, 0
    ).astype(jnp.bfloat16)
    zero_rows = jnp.zeros((8, count), jnp.bfloat16)
    table = jnp.concatenate([top_hi, zero_rows, top_lo, zero_rows, places], 0)
    for i, (ax, rel) in enumerate(routes):
        lane = rank + CAP * (back[i] % per_tile)
        wanted = (ax + 1) * 3 + shift_of(rel) + 1
        lane = jnp.where(code == wanted, lane, -1)
        choose = (first == lane).astype(F32).astype(jnp.bfloat16)
        picked = lax.dot_general(
            table, choose, (((1,), (1,)), ((), ())), preferred_element_type=F32
        )
        tile = jnp.concatenate([picked[0:24] + picked[32:56], picked[64:72]], 0)
        if (ax, rel) == (0, 0):
            item_in[back[i]] = tile
        else:
            item_out[i] = tile

    def extent(position, size):
        return 1 + (position > 0).astype(jnp.int32) + (position < size - 1).astype(jnp.int32)

    pl.semaphore_wait(barrier, extent(gx, n_gx) * extent(gy, n_gy) - 1)

    def item_copy(i):
        ax, rel = routes[i]
        return pltpu.make_async_remote_copy(
            src_ref=item_out.at[i], dst_ref=item_in.at[back[i]],
            send_sem=item_send.at[i], recv_sem=item_recv.at[back[i]],
            device_id=at(ax, shift_of(rel)), device_id_type=MESH,
        )

    for i, (ax, rel) in enumerate(routes):
        if (ax, rel) != (0, 0):
            @pl.when(here(ax, shift_of(rel)))
            def _(i=i):
                item_copy(i).start()

            @pl.when(jnp.logical_not(here(ax, shift_of(rel))))
            def _(i=i):
                item_in[i] = jnp.zeros(item_in.shape[1:], F32)

    @pl.when(jnp.logical_not(here(1, 0)))
    def _():
        later[pl.ds(0, 5), wx + 1] = jnp.zeros((5, wy, height), F32)

    @pl.when(jnp.logical_not(here(-1, 0)))
    def _():
        later[pl.ds(5, 5), 0] = jnp.zeros((5, wy, height), F32)

    corners = []
    for side, ay in ((0, 1), (1, -1)):
        for pop in Y_SETS[side]:
            if LATTICE[pop][0] != 0:
                corners.append((side, Y_SETS[side].index(pop), LATTICE[pop][0], ay))
    for side, ay in ((0, 1), (1, -1)):
        @pl.when(jnp.logical_not(here(0, ay)))
        def _(side=side):
            edge[side, :, pl.ds(8, wx), :] = jnp.zeros((5, wx, height), F32)
    for side, slot, cx, ay in corners:
        @pl.when(jnp.logical_not(here(cx, ay)))
        def _(side=side, slot=slot, cx=cx):
            edge[side, slot, pl.ds(8 + 8 * cx, 8), :] = jnp.zeros((8, height), F32)

    nothing[...] = jnp.zeros(nothing.shape, F32)
    blanks = [(out_face.at[i], nothing, cx, 0) for i, cx in enumerate((1, -1))]
    for side, ay in ((0, 1), (1, -1)):
        blanks.append((out_edge.at[side, :, pl.ds(8, wx), :], nothing.at[:, pl.ds(0, wx)], 0, ay))
    for side, slot, cx, ay in corners:
        blanks.append(
            (out_edge.at[side, slot, pl.ds(8 + 8 * cx, 8), :], nothing.at[0, pl.ds(0, 8)], cx, ay)
        )

    def blank(i):
        target, source = blanks[i][:2]
        return pltpu.make_async_copy(source, target, nothing_sem.at[i])

    for i in range(len(blanks)):
        @pl.when(jnp.logical_not(here(*blanks[i][2:])))
        def _(i=i):
            blank(i).start()

    def x_copy(stage, cx):
        pops_slot = pl.ds(0 if cx == 1 else 5, 5)
        far = wx + 1 if cx == 1 else 0
        index = 0 if cx == 1 else 1
        return pltpu.make_async_remote_copy(
            src_ref=face_out.at[stage, index],
            dst_ref=later.at[pops_slot, far] if stage == 0 else out_face.at[index],
            send_sem=face_send.at[stage, index], recv_sem=face_recv.at[stage, index],
            device_id=at(-cx, 0), device_id_type=MESH,
        )

    def y_copy(stage, side):
        target = edge if stage == 0 else out_edge
        return pltpu.make_async_remote_copy(
            src_ref=edge_out.at[stage, side], dst_ref=target.at[side, :, pl.ds(8, wx), :],
            send_sem=face_send.at[stage, 2 + side], recv_sem=face_recv.at[stage, 2 + side],
            device_id=at(0, -1 if side == 0 else 1), device_id_type=MESH,
        )

    def corner_copy(stage, number):
        side, slot, cx, ay = corners[number]
        target = edge if stage == 0 else out_edge
        return pltpu.make_async_remote_copy(
            src_ref=edge_out.at[stage, side, slot],
            dst_ref=target.at[side, slot, pl.ds(8 + 8 * cx, 8), :],
            send_sem=face_send.at[stage, 4 + number], recv_sem=face_recv.at[stage, 4 + number],
            device_id=at(-cx, -ay), device_id_type=MESH,
        )

    x_links = [(lambda stage, cx=cx: x_copy(stage, cx), cx, 0) for cx in (1, -1)]
    y_links = [(lambda stage, side=side: y_copy(stage, side), 0, 1 if side == 0 else -1) for side in (0, 1)]
    y_links += [
        (lambda stage, number=number: corner_copy(stage, number), corners[number][2], corners[number][3])
        for number in range(4)
    ]

    def start(links, stage):
        for make, cx, cy in links:
            @pl.when(here(-cx, -cy))
            def _(make=make):
                make(stage).start()

    def arrive(links, stage):
        for make, cx, cy in links:
            @pl.when(here(cx, cy))
            def _(make=make):
                make(stage).wait_recv()

    copies["pops1"].wait()
    copies["scale"].wait()

    def late(x, carry):
        velocities(pops, scale, 1, x, velocity)
        return carry

    lax.fori_loop(0, wx, late, 0, unroll=2)
    pltpu.make_async_copy(adj, later.at[:, pl.ds(1, wx)], in_sem.at[2]).wait()
    for side in range(2):
        line = 0 if side == 0 else wy - 1
        for index, pop in enumerate(Y_SETS[side]):
            for x in range(wx):
                edge_out[0, side, index, x : x + 1, :] = later[SLOT[pop], 1 + x, line : line + 1, :]

    for i, (ax, rel) in enumerate(routes):
        if (ax, rel) != (0, 0):
            @pl.when(here(ax, shift_of(rel)))
            def _(i=i):
                pltpu.make_async_remote_copy(
                    src_ref=item_out.at[i], dst_ref=item_in.at[i],
                    send_sem=item_send.at[i], recv_sem=item_recv.at[i],
                    device_id=at(ax, shift_of(rel)), device_id_type=MESH,
                ).wait_recv()

    tiles = -(-len(routes) // per_tile)
    wide = tiles * 128
    gathered = []
    for t in range(tiles):
        part = item_in[t * per_tile]
        for i in range(t * per_tile + 1, min((t + 1) * per_tile, len(routes))):
            part = part + item_in[i]
        gathered.append(part)
    items = jnp.concatenate(gathered, 1)
    hi = items.astype(jnp.bfloat16).astype(F32)
    item_all[0] = hi
    item_all[1] = items - hi
    for t in range(tiles):
        z_row = jnp.broadcast_to(gathered[t][25:26, :], (128, 128))
        z_of = z_row.T.astype(jnp.int32)
        for b in range(height // 128):
            lanes = lax.broadcasted_iota(jnp.int32, (128, 128), 1) + 128 * b
            z_hot[pl.ds(128 * t, 128), pl.ds(128 * b, 128)] = (
                (z_of == lanes).astype(F32).astype(jnp.bfloat16)
            )
    xy_of = items[24:25, :].astype(jnp.int32)

    def at_cells(length, first, stride):
        number = lax.broadcasted_iota(jnp.int32, (length, wide), 0)
        return number * stride + first == jnp.broadcast_to(xy_of, (length, wide))

    def field_of(rows):
        spread = jnp.concatenate(
            [
                jnp.where(match, item_all[part, slot : slot + 1, :], 0.0)
                for part in range(2)
                for slot, match in rows
            ],
            0,
        ).astype(jnp.bfloat16)
        both = jnp.dot(spread, z_hot[...], preferred_element_type=F32)
        half = both.shape[0] // 2
        return both[:half] + both[half:]

    near = [at_cells(wy, 0, 1), at_cells(wy, (wx - 1) * wy, 1)]
    line_of = [at_cells(wx, 0, wy), at_cells(wx, wy - 1, wy)]
    rows = [(5 * i + j, near[i]) for i in range(2) for j in range(5)]
    rows += [(SLOT[pop], line_of[side]) for side in range(2) for pop in Y_SETS[side]]
    outer = field_of(rows)
    for i in range(2):
        plane = later[pl.ds(5 * i, 5), 1 if i == 0 else wx]
        face_out[0, i] = plane + outer[5 * wy * i : 5 * wy * (i + 1)].reshape(5, wy, height)
    start(x_links, 0)
    begin = 10 * wy
    for side in range(2):
        part = outer[begin + 5 * wx * side : begin + 5 * wx * (side + 1)]
        edge_out[0, side] = edge_out[0, side] + part.reshape(5, wx, height)
    start(y_links, 0)

    def add_seeds(x, carry):
        match = at_cells(wy, x * wy, 1)
        seeds = field_of([(slot, match) for slot in range(19)])
        later[:, x + 1] = later[:, x + 1] + seeds.reshape(19, wy, height)
        return carry

    lax.fori_loop(0, wx, add_seeds, 0, unroll=4)
    copies["solid"].wait()

    def write(x):
        return pltpu.make_async_copy(middle.at[:, x], out_mid.at[:, x], out_sem.at[1 + x])

    def middle_plane(x, face=None):
        lines = {}

        def store(pop, r, c, value):
            span = pl.ds(c * 128, 128)
            middle[pop, x, pl.ds(r * 8, 8), span] = value
            cx, cy = LATTICE[pop][:2]
            if (cy == 1 and r == 0) or (cy == -1 and r == wy // 8 - 1):
                side, line = (0, 0) if cy == 1 else (1, 7)
                lines.setdefault(pop, []).append(value[line : line + 1])
                if c == height // 128 - 1:
                    whole = jnp.concatenate(lines[pop], 1)
                    edge_out[1, side, Y_SETS[side].index(pop), pl.ds(x, 1), :] = whole
            if face is not None and SLOT[pop] // 5 == face:
                face_out[1, face, SLOT[pop] % 5, pl.ds(r * 8, 8), span] = value

        adjoint_plane(later, SLOT, edge, velocity.at[1], solid, x, store)
        write(x).start()

    arrive(y_links, 0)
    arrive(x_links, 0)
    middle_plane(0, 0)
    middle_plane(wx - 1, 1)
    start(x_links, 1)

    def inner(x, carry):
        middle_plane(x)
        return carry

    lax.fori_loop(1, wx - 1, inner, 0)
    start(y_links, 1)

    copies["pops0"].wait()

    def early(x, carry):
        velocities(pops, scale, 0, x, velocity)
        return carry

    lax.fori_loop(0, wx, early, 0, unroll=2)
    velocity_write = pltpu.make_async_copy(velocity.at[0], out_velocity, out_sem.at[0])
    velocity_write.start()

    for i, (ax, rel) in enumerate(routes):
        if (ax, rel) != (0, 0):
            @pl.when(here(ax, shift_of(rel)))
            def _(i=i):
                item_copy(i).wait_send()
    for stage in range(2):
        for make, cx, cy in x_links + y_links:
            @pl.when(here(-cx, -cy))
            def _(make=make, stage=stage):
                make(stage).wait_send()
    for i in range(len(blanks)):
        @pl.when(jnp.logical_not(here(*blanks[i][2:])))
        def _(i=i):
            blank(i).wait()
    for x in range(wx):
        write(x).wait()
    velocity_write.wait()
    arrive(y_links, 1)
    arrive(x_links, 1)


def last_kernel(
    mid, face, edge_in, velocity_in, solid_in, out_init, out_mid,
    field, initial, edge, velocity, solid, side_sem, plane_sem, out_sem,
):
    wx = mid.shape[1]
    small = [
        pltpu.make_async_copy(velocity_in, velocity, side_sem.at[0]),
        pltpu.make_async_copy(solid_in, solid, side_sem.at[1]),
    ]
    for side in range(2):
        for index, pop in enumerate(Y_SETS[side]):
            cx = LATTICE[pop][0]
            span = pl.ds(0 if cx == -1 else 8, 8 if cx == 0 else 16)
            small.append(
                pltpu.make_async_copy(
                    edge_in.at[side, index, span, :], edge.at[side, index, span, :],
                    side_sem.at[2 + 5 * side + index],
                )
            )

    def face_copy(i, j):
        pop = ORDER[5 * i + j]
        return pltpu.make_async_copy(
            face.at[i, j], field.at[pop, wx + 1 if i == 0 else 0], plane_sem.at[wx + 5 * i + j]
        )

    def plane_copy(x):
        return pltpu.make_async_copy(mid.at[:, x], field.at[:, x + 1], plane_sem.at[x])

    def plane_write(x):
        return pltpu.make_async_copy(field.at[:, x + 1], out_mid.at[:, x], out_sem.at[x])

    def write(x):
        return pltpu.make_async_copy(initial.at[:, x], out_init.at[:, x], out_sem.at[wx + x])

    for j in range(5):
        face_copy(1, j).start()
    plane_copy(0).start()
    for copy in small:
        copy.start()
    for x in range(1, wx):
        plane_copy(x).start()
    for j in range(5):
        face_copy(0, j).start()

    def plane(x):
        def store(pop, r, c, value):
            initial[pop, x, pl.ds(r * 8, 8), pl.ds(c * 128, 128)] = value

        adjoint_plane(field, list(range(19)), edge, velocity, solid, x, store)
        write(x).start()

    for j in range(5):
        face_copy(1, j).wait()
    plane_copy(0).wait()
    plane_write(0).start()
    for copy in small:
        copy.wait()

    def inner(x, carry):
        plane_copy(x + 1).wait()
        plane_write(x + 1).start()
        plane(x)
        return carry

    lax.fori_loop(0, wx - 1, inner, 0)
    for j in range(5):
        face_copy(0, j).wait()
    plane(wx - 1)
    for x in range(wx):
        plane_write(x).wait()
        write(x).wait()


def body(n_gx, n_gy, adj_later, saved_pops, saved_scale, solid, seed_values, seed_contact, seed_cell):
    channels, wx, wy, height = adj_later.shape
    blocks = saved_scale.shape[-1]
    count = seed_cell.shape[0]
    scale = saved_scale.transpose(0, 2, 3, 4, 1).reshape(2, wx, wy * blocks, channels)
    routes = 6 if n_gy == 2 else 9
    wide = -(-routes * CAP // 128) * 128
    field = (channels, wx, wy, height)
    in_hbm = pl.BlockSpec(memory_space=pltpu.HBM)
    shape = lambda *dims: jax.ShapeDtypeStruct(dims, F32)
    params = dict(has_side_effects=True, vmem_limit_bytes=60 * 1024 * 1024)
    mid, face, edge, velocity = pl.pallas_call(
        functools.partial(kernel, n_gx, n_gy),
        out_shape=[
            shape(*field), shape(2, 5, wy, height), shape(2, 5, wx + 16, height),
            shape(3, wx, wy, height),
        ],
        in_specs=[in_hbm] * 7,
        out_specs=[in_hbm] * 4,
        scratch_shapes=[
            pltpu.VMEM((channels, wx + 2, wy, height), F32),
            pltpu.VMEM(field, F32),
            pltpu.VMEM((2,) + field, jnp.bfloat16),
            pltpu.VMEM(scale.shape, F32),
            pltpu.VMEM((wx, wy, height), jnp.int32),
            pltpu.VMEM((2, 3, wx, wy, height), F32),
            pltpu.VMEM((channels, count), F32),
            pltpu.VMEM((1, count), jnp.int32),
            pltpu.VMEM((1, count), jnp.int32),
            pltpu.VMEM((routes, 32, 128), F32),
            pltpu.VMEM((routes, 32, 128), F32),
            pltpu.VMEM((2, 32, wide), F32),
            pltpu.VMEM((wide, height), jnp.bfloat16),
            pltpu.VMEM((2, 2, 5, wy, height), F32),
            pltpu.VMEM((2, 2, 5, wx, height), F32),
            pltpu.VMEM((2, 5, wx + 16, height), F32),
            pltpu.VMEM((5, wy, height), F32),
            pltpu.SemaphoreType.DMA((8,)),
            pltpu.SemaphoreType.DMA((1 + wx,)),
            pltpu.SemaphoreType.DMA((8,)),
            pltpu.SemaphoreType.DMA((routes,)),
            pltpu.SemaphoreType.DMA((routes,)),
            pltpu.SemaphoreType.DMA((2, 8)),
            pltpu.SemaphoreType.DMA((2, 8)),
        ],
        compiler_params=pltpu.CompilerParams(collective_id=0, **params),
    )(
        adj_later, saved_pops, scale, solid, seed_values.T,
        seed_contact.reshape(1, count), seed_cell.reshape(1, count),
    )
    return pl.pallas_call(
        last_kernel,
        out_shape=[shape(*field)] * 2,
        in_specs=[in_hbm] * 5,
        out_specs=[in_hbm] * 2,
        scratch_shapes=[
            pltpu.VMEM((channels, wx + 2, wy, height), F32),
            pltpu.VMEM(field, F32),
            pltpu.VMEM((2, 5, wx + 16, height), F32),
            pltpu.VMEM((3, wx, wy, height), F32),
            pltpu.VMEM((wx, wy, height), jnp.int32),
            pltpu.SemaphoreType.DMA((12,)),
            pltpu.SemaphoreType.DMA((wx + 10,)),
            pltpu.SemaphoreType.DMA((2 * wx,)),
        ],
        compiler_params=pltpu.CompilerParams(vmem_limit_bytes=60 * 1024 * 1024),
    )(mid, face, edge, velocity, solid)


def solution(mesh):
    n_gx, n_gy = mesh.shape["gx"], mesh.shape["gy"]
    return jax.shard_map(
        functools.partial(body, n_gx, n_gy),
        mesh=mesh,
        in_specs=(
            P(None, "gx", "gy", None),
            P(None, None, "gx", "gy", None),
            P(None, None, "gx", "gy", None),
            P("gx", "gy", None),
            P(("gx", "gy"), None),
            P(("gx", "gy"), None),
            P(("gx", "gy")),
        ),
        out_specs=(P(None, "gx", "gy", None), P(None, "gx", "gy", None)),
        check_vma=False,
    )
```
